32 devices in a mesh: ctx: 8 (over z, core), fsdp: 4 (over y, x).
Axes of the slice: x: 2, y: 2, z: 4, core: 2. Of those that a mesh axis runs over, the one named last changes fastest.
Arguments:
- queries: bfloat16 [4096, 1024], P('ctx', 'fsdp'), may hold values from -30 to 30
- keys: bfloat16 [4096, 1024], P('ctx', 'fsdp'), may hold values from -10 to 10
- values: bfloat16 [4096, 1024], P('ctx', 'fsdp'), may hold values from -16 to 16
- norm_gain: float32 [1024], P('fsdp'), may hold values from 0.25 to 1.75
- short_filters: float32 [3, 3, 1024], P(None, None, 'fsdp'), may hold values from -3 to 3
- medium_filters: bfloat16 [128, 64], P(None, 'fsdp'), may hold values from -0.5 to 0.5
Outputs:
- mixed: bfloat16 [4096, 1024], P('ctx', 'fsdp')
The draws below stay inside these ranges and needn't reach their ends.
All inputs are finite; a program needn't handle non-finite values.
Results may differ from the reference program's by a relative error of at most 0.012.
Values may be sent and summed in bfloat16 or wider, within the bound.
A program may use at most 64 MiB of HBM per device.

```python
import math
import jax
import jax.numpy as jnp
from jax import lax

HEAD_DIM = 128
TOK_DEV = 512
TAPS = 128
SHORT = 3
GROUP_SIZE = 16
CHANNELS = 1024
SEQ = 4096
WINDOW = 1024


def draw_keys(key, part):
    base = jnp.clip(jax.random.normal(jax.random.fold_in(key, 11), (SEQ, CHANNELS), jnp.float32), -6.0, 6.0)
    return base.astype(jnp.bfloat16)


def draw_queries(key, part):
    base = jnp.clip(jax.random.normal(jax.random.fold_in(key, 13), (SEQ, CHANNELS), jnp.float32), -6.0, 6.0)
    return base.astype(jnp.bfloat16)


def draw_values(key, part):
    column = jnp.arange(CHANNELS, dtype=jnp.float32)[None, :]
    rising = 1.0 + 2.0 * column / (CHANNELS - 1)
    base = jnp.clip(jax.random.normal(jax.random.fold_in(key, 17), (SEQ, CHANNELS), jnp.float32), -5.0, 5.0)
    return (base * rising).astype(jnp.bfloat16)


def levels(key, dims, cuts, low, largest):
    def one(position, blocks):
        heights = jax.random.uniform(jax.random.fold_in(jax.random.fold_in(key, 6), position), (blocks,), jnp.float32, low / len(cuts), largest / len(cuts))
        return jnp.repeat(jnp.exp(heights), dims[position] // blocks).reshape((-1,) + (1,) * (len(dims) - position - 1))

    gain = one(*cuts[0])
    for cut in cuts[1:]:
        gain = gain * one(*cut)
    return gain


def gaussian(rng, dims, scale, reach, shards=(), kind=jnp.bfloat16):
    result = jax.random.normal(rng, dims, jnp.float32) * scale
    if len(shards) > 0:
        result = levels(rng, dims, shards, -0.22, 0.18) * result
    return jnp.clip(result, min=-reach, max=reach).astype(kind)


def setup_inputs(seed: int = 0) -> dict:
    streams_of = jax.random.split(jax.random.key(seed), 7)
    return {
        "queries": draw_queries(jax.random.fold_in(streams_of[6], 71), 0),
        "keys": draw_keys(jax.random.fold_in(streams_of[6], 71), 0),
        "values": draw_values(jax.random.fold_in(streams_of[6], 71), 0),
        "norm_gain": jnp.clip(1.0 + 0.15 * jax.random.normal(streams_of[3], (CHANNELS,), jnp.float32), 0.25, 1.75),
        "short_filters": gaussian(streams_of[4], (3, SHORT, CHANNELS), 0.6, 3.0, ((2, 4),), jnp.float32),
        "medium_filters": gaussian(streams_of[5], (TAPS, CHANNELS // GROUP_SIZE), TAPS ** -0.5, 0.5, ((1, 4),)),
    }


negative_big = -1e+30
norm_epsilon = 1e-06

def one_head(operands):
    query_head, key_head, value_head = operands
    head_size = query_head.shape[1]
    key_padded = jnp.concatenate([jnp.zeros((WINDOW, head_size), key_head.dtype), key_head], axis=0)
    value_padded = jnp.concatenate([jnp.zeros((WINDOW, head_size), value_head.dtype), value_head], axis=0)

    def one_block(block_index):
        start = (block_index * TOK_DEV).astype(jnp.int32)
        query_block = lax.dynamic_slice_in_dim(query_head, start, TOK_DEV, 0).astype(jnp.float32)
        key_block = lax.dynamic_slice_in_dim(key_padded, start, WINDOW + TOK_DEV, 0).astype(jnp.float32)
        value_block = lax.dynamic_slice_in_dim(value_padded, start, WINDOW + TOK_DEV, 0).astype(jnp.float32)
        query_pos = start + jnp.arange(TOK_DEV, dtype=jnp.int32)
        key_pos = start - WINDOW + jnp.arange(WINDOW + TOK_DEV, dtype=jnp.int32)
        allowed = (key_pos[None, :] <= query_pos[:, None]) & (key_pos[None, :] > query_pos[:, None] - WINDOW) & (key_pos[None, :] >= 0)
        scores = jnp.dot(query_block, key_block.T, precision=lax.Precision.HIGHEST) / math.sqrt(HEAD_DIM)
        masked = jnp.where(allowed, scores, negative_big)
        peak = lax.optimization_barrier(jnp.max(masked, axis=1, keepdims=True))
        exponent = jnp.where(allowed, jnp.exp(masked - peak), 0.0)
        denom = lax.optimization_barrier(jnp.sum(exponent, axis=1))
        probs = exponent.astype(jnp.bfloat16).astype(jnp.float32)
        summed = jnp.dot(probs, value_block, precision=lax.Precision.HIGHEST)
        return summed / denom[:, None]
    blocks = lax.map(one_block, jnp.arange(SEQ // TOK_DEV, dtype=jnp.int32))
    return blocks.reshape(SEQ, head_size)

def reference(queries, keys, values, norm_gain, short_filters, medium_filters):
    length, channels = queries.shape
    head_count = channels // HEAD_DIM
    query_heads = queries.reshape(length, head_count, HEAD_DIM).transpose(1, 0, 2)
    key_heads = keys.reshape(length, head_count, HEAD_DIM).transpose(1, 0, 2)
    value_heads = values.reshape(length, head_count, HEAD_DIM).transpose(1, 0, 2)
    outputs = lax.map(one_head, (query_heads, key_heads, value_heads))
    attended = outputs.transpose(1, 0, 2).reshape(length, channels).astype(jnp.bfloat16)
    attended_f = attended.astype(jnp.float32)
    mean_square = lax.optimization_barrier(jnp.mean(attended_f * attended_f, axis=1, keepdims=True))
    normed = (attended_f * lax.rsqrt(mean_square + norm_epsilon) * norm_gain[None, :]).astype(jnp.bfloat16)
    normed_f = normed.astype(jnp.float32)
    taps_short = short_filters.shape[1]
    padded = jnp.concatenate([jnp.zeros((taps_short - 1, channels), jnp.float32), normed_f], axis=0)

    def one_branch(index):
        total = jnp.zeros((length, channels), jnp.float32)
        for tap in range(taps_short):
            window = padded[taps_short - 1 - tap:taps_short - 1 - tap + length]
            total = total + short_filters[index, tap][None, :] * window
        return total
    product = (one_branch(1) * one_branch(2)).astype(jnp.bfloat16)
    product_f = product.astype(jnp.float32)
    filters_full = jnp.repeat(medium_filters.astype(jnp.float32), GROUP_SIZE, axis=1)
    taps_long = medium_filters.shape[0]
    padded_long = jnp.concatenate([jnp.zeros((taps_long - 1, channels), jnp.float32), product_f], axis=0)

    def add_tap(tap, total):
        window = lax.dynamic_slice_in_dim(padded_long, (taps_long - 1 - tap).astype(jnp.int32), length, 0)
        return total + filters_full[tap][None, :] * window
    long_mix = lax.fori_loop(0, taps_long, add_tap, jnp.zeros((length, channels), jnp.float32))
    return (attended_f + one_branch(0) * long_mix).astype(jnp.bfloat16)
```

```python
import functools
import math

import jax
import jax.numpy as jnp
from jax import lax
from jax.experimental import pallas as pl
from jax.experimental.pallas import tpu as pltpu
from jax.sharding import PartitionSpec as P

HEAD = 128
LANES = 128
QB = 256
EPS = 1e-06
BIG = -1e30
F32 = jnp.float32
BF16 = jnp.bfloat16
MESH = pl.DeviceIdType.MESH
NT = (((1,), (1,)), ((), ()))

R_Q, R_YK, R_YV, R_O, R_OS, R_HALO, R_X = 0, 1, 2, 3, 4, 5, 6


def scores_of(q_ref, k_ref, h, q0, lo, hi, mode):
    lanes = slice(h * HEAD, (h + 1) * HEAD)
    s = lax.dot_general(
        k_ref[lo:hi, lanes], q_ref[q0 : q0 + QB, lanes], NT, preferred_element_type=F32
    ) * (math.log2(math.e) / math.sqrt(HEAD))
    if mode == "full":
        return s
    key = lax.broadcasted_iota(jnp.int32, (QB, QB), 0)
    query = lax.broadcasted_iota(jnp.int32, (QB, QB), 1)
    at = q0 - lo
    allowed = key <= query if mode == "causal" else key > query
    diag = jnp.where(allowed, s[at : at + QB], BIG)
    parts = ([s[:at]] if at else []) + [diag] + ([s[at + QB :]] if at + QB < hi - lo else [])
    return jnp.concatenate(parts, axis=0) if len(parts) > 1 else diag


def block_attention(q_ref, k_ref, vt_ref, h, q0, mode, m_old):
    rows = k_ref.shape[0]
    lo, hi = {"full": (0, rows), "causal": (0, q0 + QB), "anti": (q0, rows)}[mode]
    s = scores_of(q_ref, k_ref, h, q0, lo, hi, mode)
    m = jnp.max(s, axis=0, keepdims=True)
    if m_old is not None:
        m = jnp.maximum(m, m_old)
    p = jnp.exp2(s - m)
    l = jnp.sum(p, axis=0, keepdims=True)
    o = jnp.dot(
        vt_ref[h * HEAD : (h + 1) * HEAD, lo:hi], p.astype(BF16), preferred_element_type=F32
    )
    return m, l, o


def attend(q_ref, k_ref, vt_ref, h, mode, acc, m_ref, l_ref, first=False):
    for q0 in range(0, q_ref.shape[0], QB):
        cols = slice(q0, q0 + QB)
        ch = slice(h * HEAD, (h + 1) * HEAD)
        row = slice(h, h + 1)
        m_old = None if first else m_ref[row, cols]
        m, l, o = block_attention(q_ref, k_ref, vt_ref, h, q0, mode, m_old)
        if first:
            acc[ch, cols] = o
            l_ref[row, cols] = l
        else:
            a = jnp.exp2(m_old - m)
            acc[ch, cols] = acc[ch, cols] * a + o
            l_ref[row, cols] = l_ref[row, cols] * a + l
        m_ref[row, cols] = m


def kernel(
    n_c, n_f, q, k, v, gain, sf, mf, out,
    vt, xk, xvt, yk, yvt, rq, ot, ost, rot, rost, acc, m_ref, l_ref, att, ssq, rssq,
    wide, cols_ref, toep, nrm, pext, halo, qbr, send, recv,
):
    rows, channels = q.shape
    heads = channels // HEAD
    half = heads // 2
    groups = mf.shape[1]
    size = channels // groups
    blocks = rows // LANES
    c = lax.axis_index("ctx")
    f = lax.axis_index("fsdp")
    core0 = lax.rem(c, 2) == 0
    core1 = lax.rem(c, 2) == 1
    has_prev = c >= 2
    has_next0 = core0 & (c + 2 < n_c)
    has_next1 = core1 & (c + 1 < n_c)

    def copy(src, dst, s, r, dc):
        return pltpu.make_async_remote_copy(
            src_ref=src, dst_ref=dst, send_sem=send.at[s], recv_sem=recv.at[r],
            device_id=(dc, f), device_id_type=MESH,
        )

    def x_parts(h):
        return (
            (xk.at[:, pl.ds(h * HEAD, HEAD)], k.at[:, pl.ds(h * HEAD, HEAD)]),
            (xvt.at[pl.ds(h * HEAD, HEAD)], vt.at[pl.ds(h * HEAD, HEAD)]),
        )

    def x_copy(h, kind, dc, forward):
        dst, own = x_parts(h)[kind]
        s = R_X + 2 * h + kind
        return copy(dst if forward else own, dst, s, s, dc)

    barrier = pltpu.get_barrier_semaphore()
    count = n_f - 1
    for d in range(1, n_f):
        pl.semaphore_signal(
            barrier, inc=1, device_id=(c, lax.rem(f + d, n_f)), device_id_type=MESH
        )
    for d in (1, 2):
        @pl.when(c >= d)
        def _():
            pl.semaphore_signal(barrier, inc=1, device_id=(c - d, f), device_id_type=MESH)

        @pl.when(c + d < n_c)
        def _():
            pl.semaphore_signal(barrier, inc=1, device_id=(c + d, f), device_id_type=MESH)

        count = count + jnp.where(c >= d, 1, 0) + jnp.where(c + d < n_c, 1, 0)
    pl.semaphore_wait(barrier, count)

    cp_q = copy(q, rq, R_Q, R_Q, c - 2)
    cp_yk = copy(k, yk, R_YK, R_YK, c + 1)
    cp_yv = copy(vt, yvt, R_YV, R_YV, c + 1)
    cp_o = copy(ot, rot, R_O, R_O, c + 2)
    cp_os = copy(ost, rost, R_OS, R_OS, c + 2)

    @pl.when(core0 & has_prev)
    def _():
        cp_q.start()

    def each_x(kinds, which, act):
        for h in which:
            for kind in kinds:
                act(h, kind)

    low, high = range(half), range(half, heads)

    @pl.when(has_next1)
    def _():
        each_x((0,), low, lambda h, kind: x_copy(h, kind, c + 1, False).start())
        each_x((0,), high, lambda h, kind: x_copy(h, kind, c + 2, False).start())

    @pl.when(core0)
    def _():
        cp_yk.start()

    for h in range(heads):
        for b in range(blocks):
            piece = v[b * LANES : (b + 1) * LANES, h * HEAD : (h + 1) * HEAD].astype(F32)
            vt[h * HEAD : (h + 1) * HEAD, b * LANES : (b + 1) * LANES] = piece.T.astype(BF16)

    @pl.when(has_next1)
    def _():
        each_x((1,), low, lambda h, kind: x_copy(h, kind, c + 1, False).start())
        each_x((1,), high, lambda h, kind: x_copy(h, kind, c + 2, False).start())

    @pl.when(core0)
    def _():
        cp_yv.start()

    for h in range(heads):
        attend(q, k, vt, h, "causal", acc, m_ref, l_ref, first=True)

    wide[...] = jnp.zeros_like(wide)
    for b in range(3):
        wide[3 * b : 3 * b + 3, :] = sf[b]
    wide[9:10, :] = gain[...]
    for j in range(channels // LANES):
        cols_ref[j * LANES : (j + 1) * LANES, :] = wide[:, j * LANES : (j + 1) * LANES].T
    wide[:, :groups] = mf[...].astype(F32)
    wide[:, LANES : 2 * LANES] = wide[:, :LANES].T
    e = lax.broadcasted_iota(jnp.int32, (LANES, LANES), 0)
    i = lax.broadcasted_iota(jnp.int32, (LANES, LANES), 1)
    for g in range(groups):
        taps = jnp.broadcast_to(wide[g : g + 1, LANES : 2 * LANES], (LANES, LANES))
        ring = pltpu.roll(taps, 0, 1, stride=1, stride_axis=0)
        toep[g, :LANES, :] = jnp.where(i < e, ring, 0.0).astype(BF16)
        toep[g, LANES:, :] = jnp.where(i >= e, ring, 0.0).astype(BF16)

    @pl.when(core1)
    def _():
        copy(k, yk, R_YK, R_YK, c - 1).wait_recv()
        copy(vt, yvt, R_YV, R_YV, c - 1).wait_recv()
        for h in range(heads):
            attend(q, yk, yvt, h, "full", acc, m_ref, l_ref)

    @pl.when(has_next0)
    def _():
        copy(q, rq, R_Q, R_Q, c + 2).wait_recv()
        ost[...] = jnp.zeros_like(ost)
        for h in range(heads):
            for q0 in range(0, rows, QB):
                m, l, o = block_attention(rq, k, vt, h, q0, "anti", None)
                ot[h * HEAD : (h + 1) * HEAD, q0 : q0 + QB] = (o * (1.0 / l)).astype(BF16)
                ost[h : h + 1, q0 : q0 + QB] = m
                ost[heads + h : heads + h + 1, q0 : q0 + QB] = l
        cp_o.start()
        cp_os.start()

    def far(first_heads, later_heads, other, mode):
        for h in first_heads:
            for kind in (0, 1):
                x_copy(h, kind, other, True).wait_recv()
                x_copy(h, kind, other, True).start()
        for h in first_heads:
            attend(q, xk, xvt, h, mode, acc, m_ref, l_ref)
        for h in later_heads:
            for kind in (0, 1):
                x_copy(h, kind, other, True).wait_recv()
            attend(q, xk, xvt, h, mode, acc, m_ref, l_ref)

    @pl.when(core1 & has_prev)
    def _():
        far(high, low, c - 1, "anti")

    @pl.when(core0 & has_prev)
    def _():
        far(low, high, c + 1, "full")
        copy(ot, rot, R_O, R_O, c - 2).wait_recv()
        copy(ost, rost, R_OS, R_OS, c - 2).wait_recv()
        for h in range(heads):
            ch = slice(h * HEAD, (h + 1) * HEAD)
            m_old = m_ref[h : h + 1, :]
            m_far = rost[h : h + 1, :]
            m = jnp.maximum(m_old, m_far)
            a = jnp.exp2(m_old - m)
            b = jnp.exp2(m_far - m) * rost[heads + h : heads + h + 1, :]
            acc[ch, :] = acc[ch, :] * a + rot[ch, :].astype(F32) * b
            l_ref[h : h + 1, :] = l_ref[h : h + 1, :] * a + b

    squares = jnp.zeros((1, rows), F32)
    for h in range(heads):
        ch = slice(h * HEAD, (h + 1) * HEAD)
        done = (acc[ch, :] / l_ref[h : h + 1, :]).astype(BF16)
        att[ch, :] = done
        done = done.astype(F32)
        squares = squares + jnp.sum(done * done, axis=0, keepdims=True)
    ssq[...] = jnp.broadcast_to(squares, ssq.shape)

    base = R_X + 2 * heads

    def ssq_copy(d):
        return pltpu.make_async_remote_copy(
            src_ref=ssq, dst_ref=rssq.at[d - 1], send_sem=send.at[base + d - 1],
            recv_sem=recv.at[base + d - 1],
            device_id=(c, lax.rem(f + d, n_f)), device_id_type=MESH,
        )

    for d in range(1, n_f):
        ssq_copy(d).start()
    total = ssq[0:1, :]
    for d in range(1, n_f):
        ssq_copy(d).wait_recv()
        total = total + rssq[d - 1, 0:1, :]
    scale = lax.rsqrt(total / (channels * n_f) + EPS)
    gain_col = cols_ref[:, 9:10]
    nrm[...] = (att[...].astype(F32) * scale * gain_col).astype(BF16)

    lane = lax.broadcasted_iota(jnp.int32, (channels, LANES), 1)

    def branches(b):
        here = slice(b * LANES, (b + 1) * LANES)
        now = nrm[:, here].astype(F32)
        before = halo[:, LANES:] if b == 0 else nrm[:, (b - 1) * LANES : b * LANES]
        before = before.astype(F32)
        shifted = [now]
        for t in (1, 2):
            shifted.append(
                jnp.where(lane < t, pltpu.roll(before, t, 1), pltpu.roll(now, t, 1))
            )
        total = []
        for n in range(3):
            total.append(
                sum(cols_ref[:, 3 * n + t : 3 * n + t + 1] * shifted[t] for t in range(3))
            )
        qbr[:, here] = total[0]
        return (total[1] * total[2]).astype(BF16)

    halo_src = pext.at[:, pl.ds(blocks * LANES, 2 * LANES)]
    pext[:, blocks * LANES : (blocks + 1) * LANES] = branches(blocks - 1)
    pext[:, (blocks + 1) * LANES :] = nrm[:, (blocks - 1) * LANES :]
    cp_halo = copy(halo_src, halo, R_HALO, R_HALO, c + 1)

    @pl.when(c + 1 < n_c)
    def _():
        cp_halo.start()

    for b in range(blocks - 2, 0, -1):
        pext[:, (b + 1) * LANES : (b + 2) * LANES] = branches(b)

    def mix(which):
        for g in range(groups):
            ch = slice(g * size, (g + 1) * size)
            left = jnp.concatenate(
                [pext[ch, b * LANES : (b + 2) * LANES] for b in which], axis=0
            )
            long = jnp.dot(left, toep[g], preferred_element_type=F32)
            for at, b in enumerate(which):
                here = slice(b * LANES, (b + 1) * LANES)
                acc[ch, here] = (
                    att[ch, here].astype(F32) + qbr[ch, here] * long[at * size : (at + 1) * size]
                )
        for b in which:
            for j in range(channels // LANES):
                piece = acc[j * LANES : (j + 1) * LANES, b * LANES : (b + 1) * LANES]
                out[b * LANES : (b + 1) * LANES, j * LANES : (j + 1) * LANES] = piece.T.astype(BF16)

    mix(list(range(2, blocks)))

    @pl.when(c >= 1)
    def _():
        copy(halo_src, halo, R_HALO, R_HALO, c - 1).wait_recv()

    @pl.when(c == 0)
    def _():
        halo[...] = jnp.zeros_like(halo)

    pext[:, :LANES] = halo[:, :LANES]
    pext[:, LANES : 2 * LANES] = branches(0)
    mix([0, 1])

    @pl.when(core0 & has_prev)
    def _():
        cp_q.wait_send()
        each_x((0, 1), low, lambda h, kind: x_copy(h, kind, c + 1, True).wait_send())

    @pl.when(core1 & has_prev)
    def _():
        each_x((0, 1), high, lambda h, kind: x_copy(h, kind, c - 1, True).wait_send())

    @pl.when(core0)
    def _():
        cp_yk.wait_send()
        cp_yv.wait_send()

    @pl.when(has_next0)
    def _():
        cp_o.wait_send()
        cp_os.wait_send()

    @pl.when(has_next1)
    def _():
        each_x((0, 1), low, lambda h, kind: x_copy(h, kind, c + 1, False).wait_send())
        each_x((0, 1), high, lambda h, kind: x_copy(h, kind, c + 2, False).wait_send())

    for d in range(1, n_f):
        ssq_copy(d).wait_send()

    @pl.when(c + 1 < n_c)
    def _():
        cp_halo.wait_send()


def per_device(n_c, n_f, queries, keys, values, norm_gain, short_filters, medium_filters):
    rows, channels = queries.shape
    heads = channels // HEAD
    groups = medium_filters.shape[1]
    sems = R_X + 2 * heads + n_f
    vmem = pl.BlockSpec(memory_space=pltpu.VMEM)
    long = pltpu.VMEM((rows, channels), BF16)
    turned = pltpu.VMEM((channels, rows), BF16)
    stat = pltpu.VMEM((8, rows), F32)
    return pl.pallas_call(
        functools.partial(kernel, n_c, n_f),
        out_shape=jax.ShapeDtypeStruct((rows, channels), BF16),
        in_specs=[vmem] * 6,
        out_specs=vmem,
        scratch_shapes=[
            turned, long, turned, long, turned,
            long, turned, stat, turned, stat,
            pltpu.VMEM((channels, rows), F32), stat, stat,
            turned, stat, pltpu.VMEM((n_f - 1, 8, rows), F32),
            pltpu.VMEM((LANES, channels), F32),
            pltpu.VMEM((channels, LANES), F32),
            pltpu.VMEM((groups, 2 * LANES, LANES), BF16),
            turned,
            pltpu.VMEM((channels, rows + 2 * LANES), BF16),
            pltpu.VMEM((channels, 2 * LANES), BF16),
            pltpu.VMEM((channels, rows), F32),
            pltpu.SemaphoreType.DMA((sems,)),
            pltpu.SemaphoreType.DMA((sems,)),
        ],
        compiler_params=pltpu.CompilerParams(
            collective_id=0, has_side_effects=True, vmem_limit_bytes=48 * 1024 * 1024
        ),
    )(queries, keys, values, norm_gain.reshape(1, channels), short_filters, medium_filters)


def solution(mesh):
    placed = (
        P("ctx", "fsdp"),
        P("ctx", "fsdp"),
        P("ctx", "fsdp"),
        P("fsdp"),
        P(None, None, "fsdp"),
        P(None, "fsdp"),
    )
    return jax.shard_map(
        functools.partial(per_device, mesh.shape["ctx"], mesh.shape["fsdp"]),
        mesh=mesh, in_specs=placed, out_specs=P("ctx", "fsdp"), check_vma=False,
    )
```

```python
import functools
import math

import jax
import jax.numpy as jnp
from jax import lax
from jax.experimental import pallas as pl
from jax.experimental.pallas import tpu as pltpu
from jax.sharding import PartitionSpec as P

HEAD = 128
LANES = 128
QB = 256
EPS = 1e-06
BIG = -1e30
F32 = jnp.float32
BF16 = jnp.bfloat16
MESH = pl.DeviceIdType.MESH
NT = (((1,), (1,)), ((), ()))

R_Q, R_YK, R_YV, R_HALO, R_X = 0, 1, 2, 3, 4


def scores_of(q_ref, k_ref, h, q0, lo, hi, mode):
    lanes = slice(h * HEAD, (h + 1) * HEAD)
    s = lax.dot_general(
        k_ref[lo:hi, lanes], q_ref[q0 : q0 + QB, lanes], NT, preferred_element_type=F32
    ) * (math.log2(math.e) / math.sqrt(HEAD))
    if mode == "full":
        return s
    key = lax.broadcasted_iota(jnp.int32, (QB, QB), 0)
    query = lax.broadcasted_iota(jnp.int32, (QB, QB), 1)
    at = q0 - lo
    allowed = key <= query if mode == "causal" else key > query
    diag = jnp.where(allowed, s[at : at + QB], BIG)
    parts = ([s[:at]] if at else []) + [diag] + ([s[at + QB :]] if at + QB < hi - lo else [])
    return jnp.concatenate(parts, axis=0) if len(parts) > 1 else diag


def block_attention(q_ref, k_ref, vt_ref, h, q0, mode, m_old):
    rows = k_ref.shape[0]
    lo, hi = {"full": (0, rows), "causal": (0, q0 + QB), "anti": (q0, rows)}[mode]
    s = scores_of(q_ref, k_ref, h, q0, lo, hi, mode)
    m = jnp.max(s, axis=0, keepdims=True)
    if m_old is not None:
        m = jnp.maximum(m, m_old)
    p = jnp.exp2(s - m)
    l = jnp.sum(p, axis=0, keepdims=True)
    o = jnp.dot(
        vt_ref[h * HEAD : (h + 1) * HEAD, lo:hi], p.astype(BF16), preferred_element_type=F32
    )
    return m, l, o


def attend(q_ref, k_ref, vt_ref, h, q0, mode, acc, m_ref, l_ref, first=False):
    cols = slice(q0, q0 + QB)
    ch = slice(h * HEAD, (h + 1) * HEAD)
    row = slice(h, h + 1)
    m_old = None if first else m_ref[row, cols]
    m, l, o = block_attention(q_ref, k_ref, vt_ref, h, q0, mode, m_old)
    if first:
        acc[ch, cols] = o
        l_ref[row, cols] = l
    else:
        a = jnp.exp2(m_old - m)
        acc[ch, cols] = acc[ch, cols] * a + o
        l_ref[row, cols] = l_ref[row, cols] * a + l
    m_ref[row, cols] = m


def kernel(
    n_c, n_f, q_in, k_in, v_in, gain, sf, mf, out,
    q, k, v, vt, xk, xvt, yk, yvt, rq, ot, ost, rot, rost, acc, m_ref, l_ref, att, ssq, rssq,
    wide, cols_ref, toep, nrm, pext, halo, qbr, send, recv, local,
):
    rows, channels = q.shape
    heads = channels // HEAD
    half = heads // 2
    groups = mf.shape[0]
    size = channels // groups
    blocks = rows // LANES
    n_q = rows // QB
    o_sem = R_X + 2 * heads + n_q * (n_f - 1)
    c = lax.axis_index("ctx")
    f = lax.axis_index("fsdp")
    core0 = lax.rem(c, 2) == 0
    core1 = lax.rem(c, 2) == 1
    has_prev = c >= 2
    has_next0 = core0 & (c + 2 < n_c)
    has_next1 = core1 & (c + 1 < n_c)

    def copy(src, dst, s, r, dc):
        return pltpu.make_async_remote_copy(
            src_ref=src, dst_ref=dst, send_sem=send.at[s], recv_sem=recv.at[r],
            device_id=(dc, f), device_id_type=MESH,
        )

    def x_parts(h):
        return (
            (xk.at[:, pl.ds(h * HEAD, HEAD)], k_in.at[:, pl.ds(h * HEAD, HEAD)]),
            (xvt.at[pl.ds(h * HEAD, HEAD)], vt.at[pl.ds(h * HEAD, HEAD)]),
        )

    def x_copy(h, kind, dc, forward):
        dst, own = x_parts(h)[kind]
        s = R_X + 2 * h + kind
        return copy(dst if forward else own, dst, s, s, dc)

    loads = {}
    for n, (src, dst) in enumerate(((v_in, v), (k_in, k), (q_in, q))):
        for b in range(blocks):
            piece = pl.ds(b * LANES, LANES)
            loads[n, b] = pltpu.make_async_copy(
                src.at[piece], dst.at[piece], local.at[n * blocks + b]
            )
            loads[n, b].start()

    barrier = pltpu.get_barrier_semaphore()
    count = n_f - 1
    for d in range(1, n_f):
        pl.semaphore_signal(
            barrier, inc=1, device_id=(c, lax.rem(f + d, n_f)), device_id_type=MESH
        )
    for d in (1, 2):
        @pl.when(c >= d)
        def _():
            pl.semaphore_signal(barrier, inc=1, device_id=(c - d, f), device_id_type=MESH)

        @pl.when(c + d < n_c)
        def _():
            pl.semaphore_signal(barrier, inc=1, device_id=(c + d, f), device_id_type=MESH)

        count = count + jnp.where(c >= d, 1, 0) + jnp.where(c + d < n_c, 1, 0)
    pl.semaphore_wait(barrier, count)

    cp_q = copy(q_in, rq, R_Q, R_Q, c - 2)
    cp_yk = copy(k_in, yk, R_YK, R_YK, c + 1)
    cp_yv = copy(vt, yvt, R_YV, R_YV, c + 1)

    def o_copies(n, dc):
        piece = pl.ds(n_q * QB - (n + 1) * QB, QB)
        return (
            copy(ot.at[:, piece], rot.at[:, piece], o_sem + 2 * n, o_sem + 2 * n, dc),
            copy(ost.at[:, piece], rost.at[:, piece], o_sem + 2 * n + 1, o_sem + 2 * n + 1, dc),
        )

    @pl.when(core0 & has_prev)
    def _():
        cp_q.start()

    def each_x(kinds, which, act):
        for h in which:
            for kind in kinds:
                act(h, kind)

    low, high = range(half), range(half, heads)

    @pl.when(has_next1)
    def _():
        each_x((0,), low, lambda h, kind: x_copy(h, kind, c + 1, False).start())
        each_x((0,), high, lambda h, kind: x_copy(h, kind, c + 2, False).start())

    @pl.when(core0)
    def _():
        cp_yk.start()

    for b in range(blocks):
        loads[0, b].wait()
        for h in range(heads):
            piece = v[b * LANES : (b + 1) * LANES, h * HEAD : (h + 1) * HEAD].astype(F32)
            vt[h * HEAD : (h + 1) * HEAD, b * LANES : (b + 1) * LANES] = piece.T.astype(BF16)

    @pl.when(has_next1)
    def _():
        each_x((1,), low, lambda h, kind: x_copy(h, kind, c + 1, False).start())
        each_x((1,), high, lambda h, kind: x_copy(h, kind, c + 2, False).start())

    @pl.when(core0)
    def _():
        cp_yv.start()

    for b in range(blocks):
        loads[1, b].wait()
        loads[2, b].wait()
    starts = list(range(0, rows, QB))[::-1]
    for h in range(heads):
        for q0 in starts:
            attend(q, k, vt, h, q0, "causal", acc, m_ref, l_ref, first=True)

    wide[...] = jnp.zeros_like(wide)
    for b in range(3):
        wide[3 * b : 3 * b + 3, :] = sf[b]
    wide[9:10, :] = gain[...]
    for j in range(channels // LANES):
        turned = wide[:, j * LANES : (j + 1) * LANES].T
        for n in range(10):
            cols_ref[n, j * LANES : (j + 1) * LANES, :] = jnp.broadcast_to(
                turned[:, n : n + 1], (LANES, LANES)
            )
    wide[:groups, :LANES] = mf[...].astype(F32)
    e = lax.broadcasted_iota(jnp.int32, (LANES, LANES), 0)
    i = lax.broadcasted_iota(jnp.int32, (LANES, LANES), 1)
    for g in range(groups):
        taps = jnp.broadcast_to(wide[g : g + 1, :LANES], (LANES, LANES))
        ring = pltpu.roll(taps, 0, 1, stride=1, stride_axis=0)
        side = slice(g % 2 * LANES, (g % 2 + 1) * LANES)
        toep[g // 2, :LANES, side] = jnp.where(i < e, ring, 0.0).astype(BF16)
        toep[g // 2, LANES:, side] = jnp.where(i >= e, ring, 0.0).astype(BF16)

    @pl.when(core1)
    def _():
        copy(k_in, yk, R_YK, R_YK, c - 1).wait_recv()
        copy(vt, yvt, R_YV, R_YV, c - 1).wait_recv()
        for h in range(heads):
            for q0 in starts:
                attend(q, yk, yvt, h, q0, "full", acc, m_ref, l_ref)

    @pl.when(has_next0)
    def _():
        copy(q_in, rq, R_Q, R_Q, c + 2).wait_recv()
        ost[...] = jnp.zeros_like(ost)
        for n, q0 in enumerate(starts):
            for h in range(heads):
                m, l, o = block_attention(rq, k, vt, h, q0, "anti", None)
                ot[h * HEAD : (h + 1) * HEAD, q0 : q0 + QB] = (o * (1.0 / l)).astype(BF16)
                ost[h : h + 1, q0 : q0 + QB] = m
                ost[heads + h : heads + h + 1, q0 : q0 + QB] = l
            for cp in o_copies(n, c + 2):
                cp.start()

    def far_first(first_heads, other, mode):
        for h in first_heads:
            for kind in (0, 1):
                x_copy(h, kind, other, True).wait_recv()
                x_copy(h, kind, other, True).start()
        for h in first_heads:
            for q0 in starts:
                attend(q, xk, xvt, h, q0, mode, acc, m_ref, l_ref)

    def far_later(later_heads, other, mode, n):
        for h in later_heads:
            if n == 0:
                for kind in (0, 1):
                    x_copy(h, kind, other, True).wait_recv()
            attend(q, xk, xvt, h, starts[n], mode, acc, m_ref, l_ref)

    @pl.when(core1 & has_prev)
    def _():
        far_first(high, c - 1, "anti")

    @pl.when(core0 & has_prev)
    def _():
        far_first(low, c + 1, "full")

    base = R_X + 2 * heads

    def ssq_copy(n, d):
        piece = pl.ds(starts[n], QB)
        s = base + n * (n_f - 1) + d - 1
        return pltpu.make_async_remote_copy(
            src_ref=ssq.at[:, piece], dst_ref=rssq.at[d - 1, :, piece], send_sem=send.at[s],
            recv_sem=recv.at[s], device_id=(c, lax.rem(f + d, n_f)), device_id_type=MESH,
        )

    for n, q0 in enumerate(starts):
        cols = slice(q0, q0 + QB)

        @pl.when(core1 & has_prev)
        def _():
            far_later(low, c - 1, "anti", n)

        @pl.when(core0 & has_prev)
        def _():
            far_later(high, c + 1, "full", n)
            for cp in o_copies(n, c - 2):
                cp.wait_recv()
            for h in range(heads):
                ch = slice(h * HEAD, (h + 1) * HEAD)
                m_old = m_ref[h : h + 1, cols]
                m_far = rost[h : h + 1, cols]
                m = jnp.maximum(m_old, m_far)
                a = jnp.exp2(m_old - m)
                b = jnp.exp2(m_far - m) * rost[heads + h : heads + h + 1, cols]
                acc[ch, cols] = acc[ch, cols] * a + rot[ch, cols].astype(F32) * b
                l_ref[h : h + 1, cols] = l_ref[h : h + 1, cols] * a + b

        squares = jnp.zeros((1, QB), F32)
        for h in range(heads):
            ch = slice(h * HEAD, (h + 1) * HEAD)
            done = (acc[ch, cols] * (1.0 / l_ref[h : h + 1, cols])).astype(BF16)
            att[ch, cols] = done
            done = done.astype(F32)
            squares = squares + jnp.sum(done * done, axis=0, keepdims=True)
        ssq[:, cols] = jnp.broadcast_to(squares, (8, QB))
        for d in range(1, n_f):
            ssq_copy(n, d).start()

    lane = lax.broadcasted_iota(jnp.int32, (channels, LANES), 1)

    def branches(b):
        here = slice(b * LANES, (b + 1) * LANES)
        now = nrm[:, here].astype(F32)
        before = halo[:, LANES:] if b == 0 else nrm[:, (b - 1) * LANES : b * LANES]
        before = before.astype(F32)
        shifted = [now]
        for t in (1, 2):
            shifted.append(
                jnp.where(lane < t, pltpu.roll(before, t, 1), pltpu.roll(now, t, 1))
            )
        total = []
        for n in range(3):
            total.append(sum(cols_ref[3 * n + t] * shifted[t] for t in range(3)))
        qbr[:, here] = total[0]
        pext[:, (b + 1) * LANES : (b + 2) * LANES] = (total[1] * total[2]).astype(BF16)

    halo_src = pext.at[:, pl.ds(blocks * LANES, 2 * LANES)]
    cp_halo = copy(halo_src, halo, R_HALO, R_HALO, c + 1)
    for n, q0 in enumerate(starts):
        cols = slice(q0, q0 + QB)
        total = ssq[0:1, cols]
        for d in range(1, n_f):
            ssq_copy(n, d).wait_recv()
            total = total + rssq[d - 1, 0:1, cols]
        scale = lax.rsqrt(total / (channels * n_f) + EPS)
        for b in range(q0 // LANES, (q0 + QB) // LANES):
            here = slice(b * LANES, (b + 1) * LANES)
            part = scale[:, b * LANES - q0 : (b + 1) * LANES - q0]
            nrm[:, here] = (att[:, here].astype(F32) * part * cols_ref[9]).astype(BF16)
        ready = range((q0 + QB) // LANES, q0 // LANES, -1)
        for b in ready:
            if b < blocks:
                branches(b)
            if b == blocks - 1:
                pext[:, (blocks + 1) * LANES :] = nrm[:, (blocks - 1) * LANES :]

                @pl.when(c + 1 < n_c)
                def _():
                    cp_halo.start()

    @pl.when(c >= 1)
    def _():
        copy(halo_src, halo, R_HALO, R_HALO, c - 1).wait_recv()

    @pl.when(c == 0)
    def _():
        halo[...] = jnp.zeros_like(halo)

    pext[:, :LANES] = halo[:, :LANES]
    branches(0)
    for pair in range(groups // 2):
        left = [
            pext[g * size : (g + 1) * size, b * LANES : (b + 2) * LANES]
            for g in (2 * pair, 2 * pair + 1)
            for b in range(blocks)
        ]
        long = jnp.dot(
            jnp.concatenate(left, axis=0), toep[pair], preferred_element_type=F32
        )
        for at in range(2 * blocks):
            g, b = 2 * pair + at // blocks, at % blocks
            ch = slice(g * size, (g + 1) * size)
            here = slice(b * LANES, (b + 1) * LANES)
            side = slice(at // blocks * LANES, (at // blocks + 1) * LANES)
            acc[ch, here] = (
                att[ch, here].astype(F32)
                + qbr[ch, here] * long[at * size : (at + 1) * size, side]
            )
    for j in range(channels // LANES):
        for b in range(blocks):
            piece = acc[j * LANES : (j + 1) * LANES, b * LANES : (b + 1) * LANES]
            out[b * LANES : (b + 1) * LANES, j * LANES : (j + 1) * LANES] = piece.T.astype(BF16)

    @pl.when(core0 & has_prev)
    def _():
        cp_q.wait_send()
        each_x((0, 1), low, lambda h, kind: x_copy(h, kind, c + 1, True).wait_send())

    @pl.when(core1 & has_prev)
    def _():
        each_x((0, 1), high, lambda h, kind: x_copy(h, kind, c - 1, True).wait_send())

    @pl.when(core0)
    def _():
        cp_yk.wait_send()
        cp_yv.wait_send()

    @pl.when(has_next0)
    def _():
        for n in range(n_q):
            for cp in o_copies(n, c + 2):
                cp.wait_send()

    @pl.when(has_next1)
    def _():
        each_x((0, 1), low, lambda h, kind: x_copy(h, kind, c + 1, False).wait_send())
        each_x((0, 1), high, lambda h, kind: x_copy(h, kind, c + 2, False).wait_send())

    for n in range(n_q):
        for d in range(1, n_f):
            ssq_copy(n, d).wait_send()

    @pl.when(c + 1 < n_c)
    def _():
        cp_halo.wait_send()


def per_device(n_c, n_f, queries, keys, values, norm_gain, short_filters, medium_filters):
    rows, channels = queries.shape
    heads = channels // HEAD
    groups = medium_filters.shape[1]
    sems = R_X + 2 * heads + (rows // QB) * (n_f + 1)
    hbm = pl.BlockSpec(memory_space=pltpu.HBM)
    vmem = pl.BlockSpec(memory_space=pltpu.VMEM)
    long = pltpu.VMEM((rows, channels), BF16)
    turned = pltpu.VMEM((channels, rows), BF16)
    stat = pltpu.VMEM((8, rows), F32)
    return pl.pallas_call(
        functools.partial(kernel, n_c, n_f),
        out_shape=jax.ShapeDtypeStruct((rows, channels), BF16),
        in_specs=[hbm] * 3 + [vmem] * 3,
        out_specs=vmem,
        scratch_shapes=[
            long, long, long,
            turned, long, turned, long, turned,
            long, turned, stat, turned, stat,
            pltpu.VMEM((channels, rows), F32), stat, stat,
            turned, stat, pltpu.VMEM((n_f - 1, 8, rows), F32),
            pltpu.VMEM((LANES, channels), F32),
            pltpu.VMEM((10, channels, LANES), F32),
            pltpu.VMEM((groups // 2, 2 * LANES, 2 * LANES), BF16),
            turned,
            pltpu.VMEM((channels, rows + 2 * LANES), BF16),
            pltpu.VMEM((channels, 2 * LANES), BF16),
            pltpu.VMEM((channels, rows), F32),
            pltpu.SemaphoreType.DMA((sems,)),
            pltpu.SemaphoreType.DMA((sems,)),
            pltpu.SemaphoreType.DMA((3 * rows // LANES,)),
        ],
        compiler_params=pltpu.CompilerParams(
            collective_id=0, has_side_effects=True, vmem_limit_bytes=56 * 1024 * 1024
        ),
    )(queries, keys, values, norm_gain.reshape(1, channels), short_filters, medium_filters.T)


def solution(mesh):
    placed = (
        P("ctx", "fsdp"),
        P("ctx", "fsdp"),
        P("ctx", "fsdp"),
        P("fsdp"),
        P(None, None, "fsdp"),
        P(None, "fsdp"),
    )
    return jax.shard_map(
        functools.partial(per_device, mesh.shape["ctx"], mesh.shape["fsdp"]),
        mesh=mesh, in_specs=placed, out_specs=P("ctx", "fsdp"), check_vma=False,
    )
```

```python
import functools
import math

import jax
import jax.numpy as jnp
from jax import lax
from jax.experimental import pallas as pl
from jax.experimental.pallas import tpu as pltpu
from jax.sharding import PartitionSpec as P

HEAD = 128
LANES = 128
QB = 256
EPS = 1e-06
BIG = -1e30
F32 = jnp.float32
BF16 = jnp.bfloat16
MESH = pl.DeviceIdType.MESH
NT = (((1,), (1,)), ((), ()))

R_Q, R_YK, R_YV, R_HALO, R_X = 0, 1, 2, 3, 4


def scores_of(q_ref, k_ref, h, q0, lo, hi, mode):
    lanes = slice(h * HEAD, (h + 1) * HEAD)
    s = lax.dot_general(
        k_ref[lo:hi, lanes], q_ref[q0 : q0 + QB, lanes], NT, preferred_element_type=F32
    ) * (math.log2(math.e) / math.sqrt(HEAD))
    if mode == "full":
        return s
    key = lax.broadcasted_iota(jnp.int32, (QB, QB), 0)
    query = lax.broadcasted_iota(jnp.int32, (QB, QB), 1)
    at = q0 - lo
    allowed = key <= query if mode == "causal" else key > query
    diag = jnp.where(allowed, s[at : at + QB], BIG)
    parts = ([s[:at]] if at else []) + [diag] + ([s[at + QB :]] if at + QB < hi - lo else [])
    return jnp.concatenate(parts, axis=0) if len(parts) > 1 else diag


def span(k_ref, q0, mode):
    rows = k_ref.shape[0]
    return {"full": (0, rows), "causal": (0, q0 + QB), "anti": (q0, rows)}[mode]


def pipelined(tasks):
    s = tasks[0][0]()
    for n, (_, finish) in enumerate(tasks):
        later = tasks[n + 1][0]() if n + 1 < len(tasks) else None
        finish(s)
        s = later


def softmax_task(q_ref, k_ref, vt_ref, h, q0, mode, old, write):
    lo, hi = span(k_ref, q0, mode)

    def finish(s):
        m = jnp.max(s, axis=0, keepdims=True)
        m_old = old()
        if m_old is not None:
            m = jnp.maximum(m, m_old)
        p = jnp.exp2(s - m)
        l = jnp.sum(p, axis=0, keepdims=True)
        o = jnp.dot(
            vt_ref[h * HEAD : (h + 1) * HEAD, lo:hi], p.astype(BF16), preferred_element_type=F32
        )
        write(m_old, m, l, o)

    return (lambda: scores_of(q_ref, k_ref, h, q0, lo, hi, mode)), finish


def attend(q_ref, k_ref, vt_ref, h, q0, mode, acc, m_ref, l_ref, first=False):
    cols = slice(q0, q0 + QB)
    ch = slice(h * HEAD, (h + 1) * HEAD)
    row = slice(h, h + 1)

    def write(m_old, m, l, o):
        if first:
            acc[ch, cols] = o
            l_ref[row, cols] = l
        else:
            a = jnp.exp2(m_old - m)
            acc[ch, cols] = acc[ch, cols] * a + o
            l_ref[row, cols] = l_ref[row, cols] * a + l
        m_ref[row, cols] = m

    old = (lambda: None) if first else (lambda: m_ref[row, cols])
    return softmax_task(q_ref, k_ref, vt_ref, h, q0, mode, old, write)


def kernel(
    n_c, n_f, q_in, k_in, v_in, gain, sf, mf, out,
    q, k, v, vt, xk, xvt, yk, yvt, rq, ot, ost, rot, rost, acc, m_ref, l_ref, att, ssq, rssq,
    wide, cols_ref, toep, nrm, pext, halo, qbr, send, recv, local,
):
    rows, channels = q.shape
    heads = channels // HEAD
    half = heads // 2
    groups = mf.shape[0]
    size = channels // groups
    blocks = rows // LANES
    n_q = rows // QB
    o_sem = R_X + 2 * heads + n_q * (n_f - 1)
    c = lax.axis_index("ctx")
    f = lax.axis_index("fsdp")
    core0 = lax.rem(c, 2) == 0
    core1 = lax.rem(c, 2) == 1
    has_prev = c >= 2
    has_next0 = core0 & (c + 2 < n_c)
    has_next1 = core1 & (c + 1 < n_c)

    def copy(src, dst, s, r, dc):
        return pltpu.make_async_remote_copy(
            src_ref=src, dst_ref=dst, send_sem=send.at[s], recv_sem=recv.at[r],
            device_id=(dc, f), device_id_type=MESH,
        )

    def x_parts(h):
        return (
            (xk.at[:, pl.ds(h * HEAD, HEAD)], k_in.at[:, pl.ds(h * HEAD, HEAD)]),
            (xvt.at[pl.ds(h * HEAD, HEAD)], vt.at[pl.ds(h * HEAD, HEAD)]),
        )

    def x_copy(h, kind, dc, forward):
        dst, own = x_parts(h)[kind]
        s = R_X + 2 * h + kind
        return copy(dst if forward else own, dst, s, s, dc)

    loads = {}
    for n, (src, dst) in enumerate(((v_in, v), (k_in, k), (q_in, q))):
        for b in range(blocks):
            piece = pl.ds(b * LANES, LANES)
            loads[n, b] = pltpu.make_async_copy(
                src.at[piece], dst.at[piece], local.at[n * blocks + b]
            )
            loads[n, b].start()

    barrier = pltpu.get_barrier_semaphore()
    count = n_f - 1
    for d in range(1, n_f):
        pl.semaphore_signal(
            barrier, inc=1, device_id=(c, lax.rem(f + d, n_f)), device_id_type=MESH
        )
    for d in (1, 2):
        @pl.when(c >= d)
        def _():
            pl.semaphore_signal(barrier, inc=1, device_id=(c - d, f), device_id_type=MESH)

        @pl.when(c + d < n_c)
        def _():
            pl.semaphore_signal(barrier, inc=1, device_id=(c + d, f), device_id_type=MESH)

        count = count + jnp.where(c >= d, 1, 0) + jnp.where(c + d < n_c, 1, 0)
    pl.semaphore_wait(barrier, count)

    cp_q = copy(q_in, rq, R_Q, R_Q, c - 2)
    cp_yk = copy(k_in, yk, R_YK, R_YK, c + 1)
    cp_yv = copy(vt, yvt, R_YV, R_YV, c + 1)

    def o_copies(n, dc):
        piece = pl.ds(n_q * QB - (n + 1) * QB, QB)
        return (
            copy(ot.at[:, piece], rot.at[:, piece], o_sem + 2 * n, o_sem + 2 * n, dc),
            copy(ost.at[:, piece], rost.at[:, piece], o_sem + 2 * n + 1, o_sem + 2 * n + 1, dc),
        )

    @pl.when(core0 & has_prev)
    def _():
        cp_q.start()

    def each_x(kinds, which, act):
        for h in which:
            for kind in kinds:
                act(h, kind)

    low, high = range(half), range(half, heads)

    @pl.when(has_next1)
    def _():
        each_x((0,), low, lambda h, kind: x_copy(h, kind, c + 1, False).start())
        each_x((0,), high, lambda h, kind: x_copy(h, kind, c + 2, False).start())

    @pl.when(core0)
    def _():
        cp_yk.start()

    for b in range(blocks):
        loads[0, b].wait()
        for h in range(heads):
            piece = v[b * LANES : (b + 1) * LANES, h * HEAD : (h + 1) * HEAD].astype(F32)
            vt[h * HEAD : (h + 1) * HEAD, b * LANES : (b + 1) * LANES] = piece.T.astype(BF16)

    @pl.when(has_next1)
    def _():
        each_x((1,), low, lambda h, kind: x_copy(h, kind, c + 1, False).start())
        each_x((1,), high, lambda h, kind: x_copy(h, kind, c + 2, False).start())

    @pl.when(core0)
    def _():
        cp_yv.start()

    for b in range(blocks):
        loads[1, b].wait()
        loads[2, b].wait()
    starts = list(range(0, rows, QB))[::-1]
    pipelined([
        attend(q, k, vt, h, q0, "causal", acc, m_ref, l_ref, first=True)
        for q0 in starts for h in range(heads)
    ])

    wide[...] = jnp.zeros_like(wide)
    for b in range(3):
        wide[3 * b : 3 * b + 3, :] = sf[b]
    wide[9:10, :] = gain[...]
    for j in range(channels // LANES):
        turned = wide[:, j * LANES : (j + 1) * LANES].T
        for n in range(10):
            cols_ref[n, j * LANES : (j + 1) * LANES, :] = jnp.broadcast_to(
                turned[:, n : n + 1], (LANES, LANES)
            )
    wide[:groups, :LANES] = mf[...].astype(F32)
    e = lax.broadcasted_iota(jnp.int32, (LANES, LANES), 0)
    i = lax.broadcasted_iota(jnp.int32, (LANES, LANES), 1)
    for g in range(groups):
        taps = jnp.broadcast_to(wide[g : g + 1, :LANES], (LANES, LANES))
        ring = pltpu.roll(taps, 0, 1, stride=1, stride_axis=0)
        side = slice(g % 2 * LANES, (g % 2 + 1) * LANES)
        toep[g // 2, :LANES, side] = jnp.where(i < e, ring, 0.0).astype(BF16)
        toep[g // 2, LANES:, side] = jnp.where(i >= e, ring, 0.0).astype(BF16)

    @pl.when(core1)
    def _():
        copy(k_in, yk, R_YK, R_YK, c - 1).wait_recv()
        copy(vt, yvt, R_YV, R_YV, c - 1).wait_recv()
        pipelined([
            attend(q, yk, yvt, h, q0, "full", acc, m_ref, l_ref)
            for q0 in starts for h in range(heads)
        ])

    @pl.when(has_next0)
    def _():
        copy(q_in, rq, R_Q, R_Q, c + 2).wait_recv()
        ost[...] = jnp.zeros_like(ost)

        def partial(n, h):
            cols = slice(starts[n], starts[n] + QB)

            def write(_, m, l, o):
                ot[h * HEAD : (h + 1) * HEAD, cols] = (o * (1.0 / l)).astype(BF16)
                ost[h : h + 1, cols] = m
                ost[heads + h : heads + h + 1, cols] = l
                if h == heads - 1:
                    for cp in o_copies(n, c + 2):
                        cp.start()

            return softmax_task(rq, k, vt, h, starts[n], "anti", lambda: None, write)

        pipelined([partial(n, h) for n in range(n_q) for h in range(heads)])

    def far_first(first_heads, other, mode):
        for h in first_heads:
            for kind in (0, 1):
                x_copy(h, kind, other, True).wait_recv()
                x_copy(h, kind, other, True).start()
        pipelined([
            attend(q, xk, xvt, h, q0, mode, acc, m_ref, l_ref)
            for q0 in starts for h in first_heads
        ])

    def far_later(later_heads, other, mode, n):
        for h in later_heads:
            if n == 0:
                for kind in (0, 1):
                    x_copy(h, kind, other, True).wait_recv()
        pipelined([
            attend(q, xk, xvt, h, starts[n], mode, acc, m_ref, l_ref) for h in later_heads
        ])

    @pl.when(core1 & has_prev)
    def _():
        far_first(high, c - 1, "anti")

    @pl.when(core0 & has_prev)
    def _():
        far_first(low, c + 1, "full")

    base = R_X + 2 * heads

    def ssq_copy(n, d):
        piece = pl.ds(starts[n], QB)
        s = base + n * (n_f - 1) + d - 1
        return pltpu.make_async_remote_copy(
            src_ref=ssq.at[:, piece], dst_ref=rssq.at[d - 1, :, piece], send_sem=send.at[s],
            recv_sem=recv.at[s], device_id=(c, lax.rem(f + d, n_f)), device_id_type=MESH,
        )

    for n, q0 in enumerate(starts):
        cols = slice(q0, q0 + QB)

        @pl.when(core1 & has_prev)
        def _():
            far_later(low, c - 1, "anti", n)

        @pl.when(core0 & has_prev)
        def _():
            far_later(high, c + 1, "full", n)
            for cp in o_copies(n, c - 2):
                cp.wait_recv()
            for h in range(heads):
                ch = slice(h * HEAD, (h + 1) * HEAD)
                m_old = m_ref[h : h + 1, cols]
                m_far = rost[h : h + 1, cols]
                m = jnp.maximum(m_old, m_far)
                a = jnp.exp2(m_old - m)
                b = jnp.exp2(m_far - m) * rost[heads + h : heads + h + 1, cols]
                acc[ch, cols] = acc[ch, cols] * a + rot[ch, cols].astype(F32) * b
                l_ref[h : h + 1, cols] = l_ref[h : h + 1, cols] * a + b

        squares = jnp.zeros((1, QB), F32)
        for h in range(heads):
            ch = slice(h * HEAD, (h + 1) * HEAD)
            done = (acc[ch, cols] * (1.0 / l_ref[h : h + 1, cols])).astype(BF16)
            att[ch, cols] = done
            done = done.astype(F32)
            squares = squares + jnp.sum(done * done, axis=0, keepdims=True)
        ssq[:, cols] = jnp.broadcast_to(squares, (8, QB))
        for d in range(1, n_f):
            ssq_copy(n, d).start()

    lane = lax.broadcasted_iota(jnp.int32, (channels, LANES), 1)

    def branches(b):
        here = slice(b * LANES, (b + 1) * LANES)
        now = nrm[:, here].astype(F32)
        before = halo[:, LANES:] if b == 0 else nrm[:, (b - 1) * LANES : b * LANES]
        before = before.astype(F32)
        shifted = [now]
        for t in (1, 2):
            shifted.append(
                jnp.where(lane < t, pltpu.roll(before, t, 1), pltpu.roll(now, t, 1))
            )
        total = []
        for n in range(3):
            total.append(sum(cols_ref[3 * n + t] * shifted[t] for t in range(3)))
        qbr[:, here] = total[0]
        pext[:, (b + 1) * LANES : (b + 2) * LANES] = (total[1] * total[2]).astype(BF16)

    halo_src = pext.at[:, pl.ds(blocks * LANES, 2 * LANES)]
    cp_halo = copy(halo_src, halo, R_HALO, R_HALO, c + 1)
    for n, q0 in enumerate(starts):
        cols = slice(q0, q0 + QB)
        total = ssq[0:1, cols]
        for d in range(1, n_f):
            ssq_copy(n, d).wait_recv()
            total = total + rssq[d - 1, 0:1, cols]
        scale = lax.rsqrt(total / (channels * n_f) + EPS)
        for b in range(q0 // LANES, (q0 + QB) // LANES):
            here = slice(b * LANES, (b + 1) * LANES)
            part = scale[:, b * LANES - q0 : (b + 1) * LANES - q0]
            nrm[:, here] = (att[:, here].astype(F32) * part * cols_ref[9]).astype(BF16)
        ready = range((q0 + QB) // LANES, q0 // LANES, -1)
        for b in ready:
            if b < blocks:
                branches(b)
            if b == blocks - 1:
                pext[:, (blocks + 1) * LANES :] = nrm[:, (blocks - 1) * LANES :]

                @pl.when(c + 1 < n_c)
                def _():
                    cp_halo.start()

    @pl.when(c >= 1)
    def _():
        copy(halo_src, halo, R_HALO, R_HALO, c - 1).wait_recv()

    @pl.when(c == 0)
    def _():
        halo[...] = jnp.zeros_like(halo)

    pext[:, :LANES] = halo[:, :LANES]
    branches(0)
    for pair in range(groups // 2):
        left = [
            pext[g * size : (g + 1) * size, b * LANES : (b + 2) * LANES]
            for g in (2 * pair, 2 * pair + 1)
            for b in range(blocks)
        ]
        long = jnp.dot(
            jnp.concatenate(left, axis=0), toep[pair], preferred_element_type=F32
        )
        for at in range(2 * blocks):
            g, b = 2 * pair + at // blocks, at % blocks
            ch = slice(g * size, (g + 1) * size)
            here = slice(b * LANES, (b + 1) * LANES)
            side = slice(at // blocks * LANES, (at // blocks + 1) * LANES)
            acc[ch, here] = (
                att[ch, here].astype(F32)
                + qbr[ch, here] * long[at * size : (at + 1) * size, side]
            )
        if (2 * pair + 2) * size % LANES == 0:
            j = (2 * pair + 2) * size // LANES - 1
            for b in range(blocks):
                piece = acc[j * LANES : (j + 1) * LANES, b * LANES : (b + 1) * LANES]
                out[b * LANES : (b + 1) * LANES, j * LANES : (j + 1) * LANES] = piece.T.astype(BF16)

    @pl.when(core0 & has_prev)
    def _():
        cp_q.wait_send()
        each_x((0, 1), low, lambda h, kind: x_copy(h, kind, c + 1, True).wait_send())

    @pl.when(core1 & has_prev)
    def _():
        each_x((0, 1), high, lambda h, kind: x_copy(h, kind, c - 1, True).wait_send())

    @pl.when(core0)
    def _():
        cp_yk.wait_send()
        cp_yv.wait_send()

    @pl.when(has_next0)
    def _():
        for n in range(n_q):
            for cp in o_copies(n, c + 2):
                cp.wait_send()

    @pl.when(has_next1)
    def _():
        each_x((0, 1), low, lambda h, kind: x_copy(h, kind, c + 1, False).wait_send())
        each_x((0, 1), high, lambda h, kind: x_copy(h, kind, c + 2, False).wait_send())

    for n in range(n_q):
        for d in range(1, n_f):
            ssq_copy(n, d).wait_send()

    @pl.when(c + 1 < n_c)
    def _():
        cp_halo.wait_send()


def per_device(n_c, n_f, queries, keys, values, norm_gain, short_filters, medium_filters):
    rows, channels = queries.shape
    heads = channels // HEAD
    groups = medium_filters.shape[1]
    sems = R_X + 2 * heads + (rows // QB) * (n_f + 1)
    hbm = pl.BlockSpec(memory_space=pltpu.HBM)
    vmem = pl.BlockSpec(memory_space=pltpu.VMEM)
    long = pltpu.VMEM((rows, channels), BF16)
    turned = pltpu.VMEM((channels, rows), BF16)
    stat = pltpu.VMEM((8, rows), F32)
    return pl.pallas_call(
        functools.partial(kernel, n_c, n_f),
        out_shape=jax.ShapeDtypeStruct((rows, channels), BF16),
        in_specs=[hbm] * 3 + [vmem] * 3,
        out_specs=vmem,
        scratch_shapes=[
            long, long, long,
            turned, long, turned, long, turned,
            long, turned, stat, turned, stat,
            pltpu.VMEM((channels, rows), F32), stat, stat,
            turned, stat, pltpu.VMEM((n_f - 1, 8, rows), F32),
            pltpu.VMEM((LANES, channels), F32),
            pltpu.VMEM((10, channels, LANES), F32),
            pltpu.VMEM((groups // 2, 2 * LANES, 2 * LANES), BF16),
            turned,
            pltpu.VMEM((channels, rows + 2 * LANES), BF16),
            pltpu.VMEM((channels, 2 * LANES), BF16),
            pltpu.VMEM((channels, rows), F32),
            pltpu.SemaphoreType.DMA((sems,)),
            pltpu.SemaphoreType.DMA((sems,)),
            pltpu.SemaphoreType.DMA((3 * rows // LANES,)),
        ],
        compiler_params=pltpu.CompilerParams(
            collective_id=0, has_side_effects=True, vmem_limit_bytes=54848 * 1024
        ),
    )(queries, keys, values, norm_gain.reshape(1, channels), short_filters, medium_filters.T)


def solution(mesh):
    placed = (
        P("ctx", "fsdp"),
        P("ctx", "fsdp"),
        P("ctx", "fsdp"),
        P("fsdp"),
        P(None, None, "fsdp"),
        P(None, "fsdp"),
    )
    return jax.shard_map(
        functools.partial(per_device, mesh.shape["ctx"], mesh.shape["fsdp"]),
        mesh=mesh, in_specs=placed, out_specs=P("ctx", "fsdp"), check_vma=False,
    )
```

```python
import functools
import math

import jax
import jax.numpy as jnp
from jax import lax
from jax.experimental import pallas as pl
from jax.experimental.pallas import tpu as pltpu
from jax.sharding import PartitionSpec as P

HEAD = 128
LANES = 128
QB = 256
EPS = 1e-06
BIG = -1e30
F32 = jnp.float32
BF16 = jnp.bfloat16
MESH = pl.DeviceIdType.MESH
NT = (((1,), (1,)), ((), ()))

R_Q, R_YK, R_YV, R_HALO, R_X = 0, 1, 2, 3, 4


def scores_of(q_ref, k_ref, h, q0, lo, hi, mode):
    lanes = slice(h * HEAD, (h + 1) * HEAD)
    s = lax.dot_general(
        k_ref[lo:hi, lanes], q_ref[q0 : q0 + QB, lanes], NT, preferred_element_type=F32
    ) * (math.log2(math.e) / math.sqrt(HEAD))
    if mode == "full":
        return s
    key = lax.broadcasted_iota(jnp.int32, (QB, QB), 0)
    query = lax.broadcasted_iota(jnp.int32, (QB, QB), 1)
    at = q0 - lo
    allowed = key <= query if mode == "causal" else key > query
    diag = jnp.where(allowed, s[at : at + QB], BIG)
    parts = ([s[:at]] if at else []) + [diag] + ([s[at + QB :]] if at + QB < hi - lo else [])
    return jnp.concatenate(parts, axis=0) if len(parts) > 1 else diag


def span(k_ref, q0, mode):
    rows = k_ref.shape[0]
    return {"full": (0, rows), "causal": (0, q0 + QB), "anti": (q0, rows)}[mode]


def pipelined(tasks):
    s = tasks[0][0]()
    for n, (_, finish) in enumerate(tasks):
        later = tasks[n + 1][0]() if n + 1 < len(tasks) else None
        finish(s)
        s = later


def softmax_task(q_ref, k_ref, vt_ref, h, q0, mode, old, write):
    lo, hi = span(k_ref, q0, mode)

    def finish(s):
        m = jnp.max(s, axis=0, keepdims=True)
        m_old = old()
        if m_old is not None:
            m = jnp.maximum(m, m_old)
        p = jnp.exp2(s - m)
        l = jnp.sum(p, axis=0, keepdims=True)
        o = jnp.dot(
            vt_ref[h * HEAD : (h + 1) * HEAD, lo:hi], p.astype(BF16), preferred_element_type=F32
        )
        write(m_old, m, l, o)

    return (lambda: scores_of(q_ref, k_ref, h, q0, lo, hi, mode)), finish


def attend(q_ref, k_ref, vt_ref, h, q0, mode, acc, m_ref, l_ref, first=False):
    cols = slice(q0, q0 + QB)
    ch = slice(h * HEAD, (h + 1) * HEAD)
    row = slice(h, h + 1)

    def write(m_old, m, l, o):
        if first:
            acc[ch, cols] = o
            l_ref[row, cols] = l
        else:
            a = jnp.exp2(m_old - m)
            acc[ch, cols] = acc[ch, cols] * a + o
            l_ref[row, cols] = l_ref[row, cols] * a + l
        m_ref[row, cols] = m

    old = (lambda: None) if first else (lambda: m_ref[row, cols])
    return softmax_task(q_ref, k_ref, vt_ref, h, q0, mode, old, write)


def kernel(
    n_c, n_f, q_in, k_in, v_in, gain, sf, mf, out,
    q, k, v, vt, xk, xvt, yk, yvt, rq, ot, ost, rot, rost, acc, m_ref, l_ref, att, ssq, rssq,
    wide, cols_ref, toep, nrm, pext, halo, qbr, send, recv, local,
):
    rows, channels = q.shape
    heads = channels // HEAD
    half = heads // 2
    groups = mf.shape[0]
    size = channels // groups
    blocks = rows // LANES
    n_q = rows // QB
    o_sem = R_X + 2 * heads + n_q * (n_f - 1)
    c = lax.axis_index("ctx")
    f = lax.axis_index("fsdp")
    core0 = lax.rem(c, 2) == 0
    core1 = lax.rem(c, 2) == 1
    has_prev = c >= 2
    has_next0 = core0 & (c + 2 < n_c)
    has_next1 = core1 & (c + 1 < n_c)

    def copy(src, dst, s, r, dc):
        return pltpu.make_async_remote_copy(
            src_ref=src, dst_ref=dst, send_sem=send.at[s], recv_sem=recv.at[r],
            device_id=(dc, f), device_id_type=MESH,
        )

    def x_parts(h):
        return (
            (xk.at[:, pl.ds(h * HEAD, HEAD)], k_in.at[:, pl.ds(h * HEAD, HEAD)]),
            (xvt.at[pl.ds(h * HEAD, HEAD)], vt.at[pl.ds(h * HEAD, HEAD)]),
        )

    def x_copy(h, kind, dc, forward):
        dst, own = x_parts(h)[kind]
        s = R_X + 2 * h + kind
        return copy(dst if forward else own, dst, s, s, dc)

    loads = {}
    for n, (src, dst) in enumerate(((v_in, v), (k_in, k), (q_in, q))):
        for b in range(blocks):
            piece = pl.ds(b * LANES, LANES)
            loads[n, b] = pltpu.make_async_copy(
                src.at[piece], dst.at[piece], local.at[n * blocks + b]
            )
            loads[n, b].start()

    barrier = pltpu.get_barrier_semaphore()
    count = n_f - 1
    for d in range(1, n_f):
        pl.semaphore_signal(
            barrier, inc=1, device_id=(c, lax.rem(f + d, n_f)), device_id_type=MESH
        )
    for d in (1, 2):
        @pl.when(c >= d)
        def _():
            pl.semaphore_signal(barrier, inc=1, device_id=(c - d, f), device_id_type=MESH)

        @pl.when(c + d < n_c)
        def _():
            pl.semaphore_signal(barrier, inc=1, device_id=(c + d, f), device_id_type=MESH)

        count = count + jnp.where(c >= d, 1, 0) + jnp.where(c + d < n_c, 1, 0)
    pl.semaphore_wait(barrier, count)

    cp_q = copy(q_in, rq, R_Q, R_Q, c - 2)
    cp_yk = copy(k_in, yk, R_YK, R_YK, c + 1)
    cp_yv = copy(vt, yvt, R_YV, R_YV, c + 1)

    def o_copies(n, dc):
        piece = pl.ds(n_q * QB - (n + 1) * QB, QB)
        return (
            copy(ot.at[:, piece], rot.at[:, piece], o_sem + 2 * n, o_sem + 2 * n, dc),
            copy(ost.at[:, piece], rost.at[:, piece], o_sem + 2 * n + 1, o_sem + 2 * n + 1, dc),
        )

    @pl.when(core0 & has_prev)
    def _():
        cp_q.start()

    def each_x(kinds, which, act):
        for h in which:
            for kind in kinds:
                act(h, kind)

    low, high = range(half), range(half, heads)

    @pl.when(has_next1)
    def _():
        each_x((0,), low, lambda h, kind: x_copy(h, kind, c + 1, False).start())
        each_x((0,), high, lambda h, kind: x_copy(h, kind, c + 2, False).start())

    @pl.when(core0)
    def _():
        cp_yk.start()

    for b in range(blocks):
        loads[0, b].wait()
        for h in range(heads):
            piece = v[b * LANES : (b + 1) * LANES, h * HEAD : (h + 1) * HEAD].astype(F32)
            vt[h * HEAD : (h + 1) * HEAD, b * LANES : (b + 1) * LANES] = piece.T.astype(BF16)

    @pl.when(has_next1)
    def _():
        each_x((1,), low, lambda h, kind: x_copy(h, kind, c + 1, False).start())
        each_x((1,), high, lambda h, kind: x_copy(h, kind, c + 2, False).start())

    @pl.when(core0)
    def _():
        cp_yv.start()

    for b in range(blocks):
        loads[1, b].wait()
        loads[2, b].wait()
    starts = list(range(0, rows, QB))[::-1]
    pipelined([
        attend(q, k, vt, h, q0, "causal", acc, m_ref, l_ref, first=True)
        for q0 in starts for h in range(heads)
    ])

    wide[...] = jnp.zeros_like(wide)
    for b in range(3):
        wide[3 * b : 3 * b + 3, :] = sf[b]
    wide[9:10, :] = gain[...]
    for j in range(channels // LANES):
        turned = wide[:, j * LANES : (j + 1) * LANES].T
        for n in range(10):
            cols_ref[n, j * LANES : (j + 1) * LANES, :] = jnp.broadcast_to(
                turned[:, n : n + 1], (LANES, LANES)
            )
    wide[:groups, :LANES] = mf[...].astype(F32)
    e = lax.broadcasted_iota(jnp.int32, (LANES, LANES), 0)
    i = lax.broadcasted_iota(jnp.int32, (LANES, LANES), 1)
    for g in range(groups):
        taps = jnp.broadcast_to(wide[g : g + 1, :LANES], (LANES, LANES))
        ring = pltpu.roll(taps, 0, 1, stride=1, stride_axis=0)
        side = slice(g % 2 * LANES, (g % 2 + 1) * LANES)
        toep[g // 2, :LANES, side] = jnp.where(i < e, ring, 0.0).astype(BF16)
        toep[g // 2, LANES:, side] = jnp.where(i >= e, ring, 0.0).astype(BF16)

    @pl.when(core1)
    def _():
        copy(k_in, yk, R_YK, R_YK, c - 1).wait_recv()
        copy(vt, yvt, R_YV, R_YV, c - 1).wait_recv()
        pipelined([
            attend(q, yk, yvt, h, q0, "full", acc, m_ref, l_ref)
            for q0 in starts for h in range(heads)
        ])

    @pl.when(has_next0)
    def _():
        copy(q_in, rq, R_Q, R_Q, c + 2).wait_recv()
        ost[...] = jnp.zeros_like(ost)

        def partial(n, h):
            cols = slice(starts[n], starts[n] + QB)

            def write(_, m, l, o):
                ot[h * HEAD : (h + 1) * HEAD, cols] = (o * (1.0 / l)).astype(BF16)
                ost[h : h + 1, cols] = m
                ost[heads + h : heads + h + 1, cols] = l
                if h == heads - 1:
                    for cp in o_copies(n, c + 2):
                        cp.start()

            return softmax_task(rq, k, vt, h, starts[n], "anti", lambda: None, write)

        pipelined([partial(n, h) for n in range(n_q) for h in range(heads)])

    def far_first(first_heads, other, mode, n):
        if n == 0:
            for h in first_heads:
                for kind in (0, 1):
                    x_copy(h, kind, other, True).wait_recv()
                    x_copy(h, kind, other, True).start()
        pipelined([
            attend(q, xk, xvt, h, starts[n], mode, acc, m_ref, l_ref) for h in first_heads
        ])

    def far_later(later_heads, other, mode, n):
        if n == 0:
            for h in later_heads:
                for kind in (0, 1):
                    x_copy(h, kind, other, True).wait_recv()
        pipelined([
            attend(q, xk, xvt, h, starts[n], mode, acc, m_ref, l_ref) for h in later_heads
        ])

    base = R_X + 2 * heads

    def ssq_copy(n, d):
        piece = pl.ds(starts[n], QB)
        s = base + n * (n_f - 1) + d - 1
        return pltpu.make_async_remote_copy(
            src_ref=ssq.at[:, piece], dst_ref=rssq.at[d - 1, :, piece], send_sem=send.at[s],
            recv_sem=recv.at[s], device_id=(c, lax.rem(f + d, n_f)), device_id_type=MESH,
        )

    lane = lax.broadcasted_iota(jnp.int32, (channels, LANES), 1)

    def branches(b):
        here = slice(b * LANES, (b + 1) * LANES)
        now = nrm[:, here].astype(F32)
        before = halo[:, LANES:] if b == 0 else nrm[:, (b - 1) * LANES : b * LANES]
        before = before.astype(F32)
        shifted = [now]
        for t in (1, 2):
            shifted.append(
                jnp.where(lane < t, pltpu.roll(before, t, 1), pltpu.roll(now, t, 1))
            )
        total = []
        for n in range(3):
            total.append(sum(cols_ref[3 * n + t] * shifted[t] for t in range(3)))
        qbr[:, here] = total[0]
        pext[:, (b + 1) * LANES : (b + 2) * LANES] = (total[1] * total[2]).astype(BF16)

    halo_src = pext.at[:, pl.ds(blocks * LANES, 2 * LANES)]
    cp_halo = copy(halo_src, halo, R_HALO, R_HALO, c + 1)
    def normalise(n):
        q0 = starts[n]
        cols = slice(q0, q0 + QB)
        total = ssq[0:1, cols]
        for d in range(1, n_f):
            ssq_copy(n, d).wait_recv()
            total = total + rssq[d - 1, 0:1, cols]
        scale = lax.rsqrt(total / (channels * n_f) + EPS)
        for b in range(q0 // LANES, (q0 + QB) // LANES):
            here = slice(b * LANES, (b + 1) * LANES)
            part = scale[:, b * LANES - q0 : (b + 1) * LANES - q0]
            nrm[:, here] = (att[:, here].astype(F32) * part * cols_ref[9]).astype(BF16)
        ready = range((q0 + QB) // LANES, q0 // LANES, -1)
        for b in ready:
            if b < blocks:
                branches(b)
            if b == blocks - 1:
                pext[:, (blocks + 1) * LANES :] = nrm[:, (blocks - 1) * LANES :]

                @pl.when(c + 1 < n_c)
                def _():
                    cp_halo.start()

    for n, q0 in enumerate(starts):
        cols = slice(q0, q0 + QB)

        @pl.when(core1 & has_prev)
        def _():
            far_first(high, c - 1, "anti", n)

        @pl.when(core0 & has_prev)
        def _():
            far_first(low, c + 1, "full", n)

        if n > 0:
            normalise(n - 1)

        @pl.when(core1 & has_prev)
        def _():
            far_later(low, c - 1, "anti", n)

        @pl.when(core0 & has_prev)
        def _():
            far_later(high, c + 1, "full", n)
            for cp in o_copies(n, c - 2):
                cp.wait_recv()
            for h in range(heads):
                ch = slice(h * HEAD, (h + 1) * HEAD)
                m_old = m_ref[h : h + 1, cols]
                m_far = rost[h : h + 1, cols]
                m = jnp.maximum(m_old, m_far)
                a = jnp.exp2(m_old - m)
                b = jnp.exp2(m_far - m) * rost[heads + h : heads + h + 1, cols]
                acc[ch, cols] = acc[ch, cols] * a + rot[ch, cols].astype(F32) * b
                l_ref[h : h + 1, cols] = l_ref[h : h + 1, cols] * a + b

        squares = jnp.zeros((1, QB), F32)
        for h in range(heads):
            ch = slice(h * HEAD, (h + 1) * HEAD)
            done = (acc[ch, cols] * (1.0 / l_ref[h : h + 1, cols])).astype(BF16)
            att[ch, cols] = done
            done = done.astype(F32)
            squares = squares + jnp.sum(done * done, axis=0, keepdims=True)
        ssq[:, cols] = jnp.broadcast_to(squares, (8, QB))
        for d in range(1, n_f):
            ssq_copy(n, d).start()

    normalise(n_q - 1)

    @pl.when(c >= 1)
    def _():
        copy(halo_src, halo, R_HALO, R_HALO, c - 1).wait_recv()

    @pl.when(c == 0)
    def _():
        halo[...] = jnp.zeros_like(halo)

    pext[:, :LANES] = halo[:, :LANES]
    branches(0)
    for pair in range(groups // 2):
        left = [
            pext[g * size : (g + 1) * size, b * LANES : (b + 2) * LANES]
            for g in (2 * pair, 2 * pair + 1)
            for b in range(blocks)
        ]
        long = jnp.dot(
            jnp.concatenate(left, axis=0), toep[pair], preferred_element_type=F32
        )
        for at in range(2 * blocks):
            g, b = 2 * pair + at // blocks, at % blocks
            ch = slice(g * size, (g + 1) * size)
            here = slice(b * LANES, (b + 1) * LANES)
            side = slice(at // blocks * LANES, (at // blocks + 1) * LANES)
            acc[ch, here] = (
                att[ch, here].astype(F32)
                + qbr[ch, here] * long[at * size : (at + 1) * size, side]
            )
        if (2 * pair + 2) * size % LANES == 0:
            j = (2 * pair + 2) * size // LANES - 1
            for b in range(blocks):
                piece = acc[j * LANES : (j + 1) * LANES, b * LANES : (b + 1) * LANES]
                out[b * LANES : (b + 1) * LANES, j * LANES : (j + 1) * LANES] = piece.T.astype(BF16)

    @pl.when(core0 & has_prev)
    def _():
        cp_q.wait_send()
        each_x((0, 1), low, lambda h, kind: x_copy(h, kind, c + 1, True).wait_send())

    @pl.when(core1 & has_prev)
    def _():
        each_x((0, 1), high, lambda h, kind: x_copy(h, kind, c - 1, True).wait_send())

    @pl.when(core0)
    def _():
        cp_yk.wait_send()
        cp_yv.wait_send()

    @pl.when(has_next0)
    def _():
        for n in range(n_q):
            for cp in o_copies(n, c + 2):
                cp.wait_send()

    @pl.when(has_next1)
    def _():
        each_x((0, 1), low, lambda h, kind: x_copy(h, kind, c + 1, False).wait_send())
        each_x((0, 1), high, lambda h, kind: x_copy(h, kind, c + 2, False).wait_send())

    for n in range(n_q):
        for d in range(1, n_f):
            ssq_copy(n, d).wait_send()

    @pl.when(c + 1 < n_c)
    def _():
        cp_halo.wait_send()


def per_device(n_c, n_f, queries, keys, values, norm_gain, short_filters, medium_filters):
    rows, channels = queries.shape
    heads = channels // HEAD
    groups = medium_filters.shape[1]
    sems = R_X + 2 * heads + (rows // QB) * (n_f + 1)
    hbm = pl.BlockSpec(memory_space=pltpu.HBM)
    vmem = pl.BlockSpec(memory_space=pltpu.VMEM)
    long = pltpu.VMEM((rows, channels), BF16)
    turned = pltpu.VMEM((channels, rows), BF16)
    stat = pltpu.VMEM((8, rows), F32)
    return pl.pallas_call(
        functools.partial(kernel, n_c, n_f),
        out_shape=jax.ShapeDtypeStruct((rows, channels), BF16),
        in_specs=[hbm] * 3 + [vmem] * 3,
        out_specs=vmem,
        scratch_shapes=[
            long, long, long,
            turned, long, turned, long, turned,
            long, turned, stat, turned, stat,
            pltpu.VMEM((channels, rows), F32), stat, stat,
            turned, stat, pltpu.VMEM((n_f - 1, 8, rows), F32),
            pltpu.VMEM((LANES, channels), F32),
            pltpu.VMEM((10, channels, LANES), F32),
            pltpu.VMEM((groups // 2, 2 * LANES, 2 * LANES), BF16),
            turned,
            pltpu.VMEM((channels, rows + 2 * LANES), BF16),
            pltpu.VMEM((channels, 2 * LANES), BF16),
            pltpu.VMEM((channels, rows), F32),
            pltpu.SemaphoreType.DMA((sems,)),
            pltpu.SemaphoreType.DMA((sems,)),
            pltpu.SemaphoreType.DMA((3 * rows // LANES,)),
        ],
        compiler_params=pltpu.CompilerParams(
            collective_id=0, has_side_effects=True, vmem_limit_bytes=56320 * 1024
        ),
    )(queries, keys, values, norm_gain.reshape(1, channels), short_filters, medium_filters.T)


def solution(mesh):
    placed = (
        P("ctx", "fsdp"),
        P("ctx", "fsdp"),
        P("ctx", "fsdp"),
        P("fsdp"),
        P(None, None, "fsdp"),
        P(None, "fsdp"),
    )
    return jax.shard_map(
        functools.partial(per_device, mesh.shape["ctx"], mesh.shape["fsdp"]),
        mesh=mesh, in_specs=placed, out_specs=P("ctx", "fsdp"), check_vma=False,
    )
```

```python
import functools
import math

import jax
import jax.numpy as jnp
from jax import lax
from jax.experimental import pallas as pl
from jax.experimental.pallas import tpu as pltpu
from jax.sharding import PartitionSpec as P

HEAD = 128
LANES = 128
QB = 256
EPS = 1e-06
BIG = -1e30
F32 = jnp.float32
BF16 = jnp.bfloat16
MESH = pl.DeviceIdType.MESH
NT = (((1,), (1,)), ((), ()))

R_Q, R_YK, R_YV, R_HALO, R_X = 0, 1, 2, 3, 4


def scores_of(q_ref, k_ref, h, q0, lo, hi, mode):
    lanes = slice(h * HEAD, (h + 1) * HEAD)
    s = lax.dot_general(
        k_ref[lo:hi, lanes], q_ref[q0 : q0 + QB, lanes], NT, preferred_element_type=F32
    ) * (math.log2(math.e) / math.sqrt(HEAD))
    if mode == "full":
        return s
    key = lax.broadcasted_iota(jnp.int32, (QB, QB), 0)
    query = lax.broadcasted_iota(jnp.int32, (QB, QB), 1)
    at = q0 - lo
    allowed = key <= query if mode == "causal" else key > query
    diag = jnp.where(allowed, s[at : at + QB], BIG)
    parts = ([s[:at]] if at else []) + [diag] + ([s[at + QB :]] if at + QB < hi - lo else [])
    return jnp.concatenate(parts, axis=0) if len(parts) > 1 else diag


def span(k_ref, q0, mode):
    rows = k_ref.shape[0]
    return {"full": (0, rows), "causal": (0, q0 + QB), "anti": (q0, rows)}[mode]


def pipelined(tasks):
    s = tasks[0][0]()
    for n, (_, finish) in enumerate(tasks):
        later = tasks[n + 1][0]() if n + 1 < len(tasks) else None
        finish(s)
        s = later


def softmax_task(q_ref, k_ref, vt_ref, h, q0, mode, old, write):
    lo, hi = span(k_ref, q0, mode)

    def finish(s):
        m = jnp.max(s, axis=0, keepdims=True)
        m_old = old()
        if m_old is not None:
            m = jnp.maximum(m, m_old)
        p = jnp.exp2(s - m)
        l = jnp.sum(p, axis=0, keepdims=True)
        o = jnp.dot(
            vt_ref[h * HEAD : (h + 1) * HEAD, lo:hi], p.astype(BF16), preferred_element_type=F32
        )
        write(m_old, m, l, o)

    return (lambda: scores_of(q_ref, k_ref, h, q0, lo, hi, mode)), finish


def attend(q_ref, k_ref, vt_ref, h, q0, mode, acc, m_ref, l_ref, first=False):
    cols = slice(q0, q0 + QB)
    ch = slice(h * HEAD, (h + 1) * HEAD)
    row = slice(h, h + 1)

    def write(m_old, m, l, o):
        if first:
            acc[ch, cols] = o
            l_ref[row, cols] = l
        else:
            a = jnp.exp2(m_old - m)
            acc[ch, cols] = acc[ch, cols] * a + o
            l_ref[row, cols] = l_ref[row, cols] * a + l
        m_ref[row, cols] = m

    old = (lambda: None) if first else (lambda: m_ref[row, cols])
    return softmax_task(q_ref, k_ref, vt_ref, h, q0, mode, old, write)


def kernel(
    n_c, n_f, q_in, k_in, v_in, gain, sf, mf, out,
    q, k, v, vt, xk, xvt, yk, yvt, rq, ot, ost, rot, rost, acc, m_ref, l_ref, att, ssq, rssq,
    wide, cols_ref, toep, nrm, pext, halo, qbr, send, recv, local,
):
    rows, channels = q.shape
    heads = channels // HEAD
    half = heads // 2
    groups = mf.shape[0]
    size = channels // groups
    blocks = rows // LANES
    n_q = rows // QB
    o_sem = R_X + 2 * heads + n_q * (n_f - 1)
    c = lax.axis_index("ctx")
    f = lax.axis_index("fsdp")
    core0 = lax.rem(c, 2) == 0
    core1 = lax.rem(c, 2) == 1
    has_prev = c >= 2
    has_next0 = core0 & (c + 2 < n_c)
    has_next1 = core1 & (c + 1 < n_c)

    def copy(src, dst, s, r, dc):
        return pltpu.make_async_remote_copy(
            src_ref=src, dst_ref=dst, send_sem=send.at[s], recv_sem=recv.at[r],
            device_id=(dc, f), device_id_type=MESH,
        )

    def x_parts(h):
        return (
            (xk.at[:, pl.ds(h * HEAD, HEAD)], k_in.at[:, pl.ds(h * HEAD, HEAD)]),
            (xvt.at[pl.ds(h * HEAD, HEAD)], vt.at[pl.ds(h * HEAD, HEAD)]),
        )

    def x_copy(h, kind, dc, forward):
        dst, own = x_parts(h)[kind]
        s = R_X + 2 * h + kind
        return copy(dst if forward else own, dst, s, s, dc)

    loads = {}
    for n, (src, dst) in enumerate(((v_in, v), (k_in, k), (q_in, q))):
        for b in range(blocks):
            piece = pl.ds(b * LANES, LANES)
            loads[n, b] = pltpu.make_async_copy(
                src.at[piece], dst.at[piece], local.at[n * blocks + b]
            )
            loads[n, b].start()

    barrier = pltpu.get_barrier_semaphore()
    count = n_f - 1
    for d in range(1, n_f):
        pl.semaphore_signal(
            barrier, inc=1, device_id=(c, lax.rem(f + d, n_f)), device_id_type=MESH
        )
    for d in (1, 2):
        @pl.when(c >= d)
        def _():
            pl.semaphore_signal(barrier, inc=1, device_id=(c - d, f), device_id_type=MESH)

        @pl.when(c + d < n_c)
        def _():
            pl.semaphore_signal(barrier, inc=1, device_id=(c + d, f), device_id_type=MESH)

        count = count + jnp.where(c >= d, 1, 0) + jnp.where(c + d < n_c, 1, 0)
    pl.semaphore_wait(barrier, count)

    cp_q = copy(q_in, rq, R_Q, R_Q, c - 2)
    cp_yk = copy(k_in, yk, R_YK, R_YK, c + 1)
    cp_yv = copy(vt, yvt, R_YV, R_YV, c + 1)

    def o_copies(n, dc):
        piece = pl.ds(n_q * QB - (n + 1) * QB, QB)
        return (
            copy(ot.at[:, piece], rot.at[:, piece], o_sem + 2 * n, o_sem + 2 * n, dc),
            copy(ost.at[:, piece], rost.at[:, piece], o_sem + 2 * n + 1, o_sem + 2 * n + 1, dc),
        )

    @pl.when(core0 & has_prev)
    def _():
        cp_q.start()

    def each_x(kinds, which, act):
        for h in which:
            for kind in kinds:
                act(h, kind)

    low, high = range(half), range(half, heads)

    @pl.when(has_next1)
    def _():
        each_x((0,), low, lambda h, kind: x_copy(h, kind, c + 1, False).start())
        each_x((0,), high, lambda h, kind: x_copy(h, kind, c + 2, False).start())

    @pl.when(core0)
    def _():
        cp_yk.start()

    for b in range(blocks):
        loads[0, b].wait()
        for h in range(heads):
            piece = v[b * LANES : (b + 1) * LANES, h * HEAD : (h + 1) * HEAD].astype(F32)
            vt[h * HEAD : (h + 1) * HEAD, b * LANES : (b + 1) * LANES] = piece.T.astype(BF16)

    @pl.when(has_next1)
    def _():
        each_x((1,), low, lambda h, kind: x_copy(h, kind, c + 1, False).start())
        each_x((1,), high, lambda h, kind: x_copy(h, kind, c + 2, False).start())

    @pl.when(core0)
    def _():
        cp_yv.start()

    for b in range(blocks):
        loads[1, b].wait()
        loads[2, b].wait()
    starts = list(range(0, rows, QB))[::-1]
    pipelined([
        attend(q, k, vt, h, q0, "causal", acc, m_ref, l_ref, first=True)
        for q0 in starts for h in range(heads)
    ])

    wide[...] = jnp.zeros_like(wide)
    for b in range(3):
        wide[3 * b : 3 * b + 3, :] = sf[b]
    wide[9:10, :] = gain[...]
    for j in range(channels // LANES):
        turned = wide[:, j * LANES : (j + 1) * LANES].T
        for n in range(10):
            cols_ref[n, j * LANES : (j + 1) * LANES, :] = jnp.broadcast_to(
                turned[:, n : n + 1], (LANES, LANES)
            )
    wide[:groups, :LANES] = mf[...].astype(F32)
    e = lax.broadcasted_iota(jnp.int32, (LANES, LANES), 0)
    i = lax.broadcasted_iota(jnp.int32, (LANES, LANES), 1)
    for g in range(groups):
        taps = jnp.broadcast_to(wide[g : g + 1, :LANES], (LANES, LANES))
        ring = pltpu.roll(taps, 0, 1, stride=1, stride_axis=0)
        side = slice(g % 2 * LANES, (g % 2 + 1) * LANES)
        toep[g // 2, :LANES, side] = jnp.where(i < e, ring, 0.0).astype(BF16)
        toep[g // 2, LANES:, side] = jnp.where(i >= e, ring, 0.0).astype(BF16)

    @pl.when(core1)
    def _():
        copy(k_in, yk, R_YK, R_YK, c - 1).wait_recv()
        copy(vt, yvt, R_YV, R_YV, c - 1).wait_recv()
        pipelined([
            attend(q, yk, yvt, h, q0, "full", acc, m_ref, l_ref)
            for q0 in starts for h in range(heads)
        ])

    @pl.when(has_next0)
    def _():
        copy(q_in, rq, R_Q, R_Q, c + 2).wait_recv()
        ost[...] = jnp.zeros_like(ost)

        def partial(n, h):
            cols = slice(starts[n], starts[n] + QB)

            def write(_, m, l, o):
                ot[h * HEAD : (h + 1) * HEAD, cols] = (o * (1.0 / l)).astype(BF16)
                ost[h : h + 1, cols] = m
                ost[heads + h : heads + h + 1, cols] = l
                if h == heads - 1:
                    for cp in o_copies(n, c + 2):
                        cp.start()

            return softmax_task(rq, k, vt, h, starts[n], "anti", lambda: None, write)

        pipelined([partial(n, h) for n in range(n_q) for h in range(heads)])

    def far_first(first_heads, other, mode):
        for h in first_heads:
            for kind in (0, 1):
                x_copy(h, kind, other, True).wait_recv()
                x_copy(h, kind, other, True).start()
        pipelined([
            attend(q, xk, xvt, h, q0, mode, acc, m_ref, l_ref)
            for q0 in starts for h in first_heads
        ])

    def far_later(later_heads, other, mode, n):
        for h in later_heads:
            if n == 0:
                for kind in (0, 1):
                    x_copy(h, kind, other, True).wait_recv()
        pipelined([
            attend(q, xk, xvt, h, starts[n], mode, acc, m_ref, l_ref) for h in later_heads
        ])

    @pl.when(core1 & has_prev)
    def _():
        far_first(high, c - 1, "anti")

    @pl.when(core0 & has_prev)
    def _():
        far_first(low, c + 1, "full")

    base = R_X + 2 * heads

    def ssq_copy(n, d):
        piece = pl.ds(starts[n], QB)
        s = base + n * (n_f - 1) + d - 1
        return pltpu.make_async_remote_copy(
            src_ref=ssq.at[:, piece], dst_ref=rssq.at[d - 1, :, piece], send_sem=send.at[s],
            recv_sem=recv.at[s], device_id=(c, lax.rem(f + d, n_f)), device_id_type=MESH,
        )

    for n, q0 in enumerate(starts):
        cols = slice(q0, q0 + QB)

        @pl.when(core1 & has_prev)
        def _():
            far_later(low, c - 1, "anti", n)

        @pl.when(core0 & has_prev)
        def _():
            far_later(high, c + 1, "full", n)
            for cp in o_copies(n, c - 2):
                cp.wait_recv()
            for h in range(heads):
                ch = slice(h * HEAD, (h + 1) * HEAD)
                m_old = m_ref[h : h + 1, cols]
                m_far = rost[h : h + 1, cols]
                m = jnp.maximum(m_old, m_far)
                a = jnp.exp2(m_old - m)
                b = jnp.exp2(m_far - m) * rost[heads + h : heads + h + 1, cols]
                acc[ch, cols] = acc[ch, cols] * a + rot[ch, cols].astype(F32) * b
                l_ref[h : h + 1, cols] = l_ref[h : h + 1, cols] * a + b

        squares = jnp.zeros((1, QB), F32)
        for h in range(heads):
            ch = slice(h * HEAD, (h + 1) * HEAD)
            done = (acc[ch, cols] * (1.0 / l_ref[h : h + 1, cols])).astype(BF16)
            att[ch, cols] = done
            done = done.astype(F32)
            squares = squares + jnp.sum(done * done, axis=0, keepdims=True)
        ssq[:, cols] = jnp.broadcast_to(squares, (8, QB))
        for d in range(1, n_f):
            ssq_copy(n, d).start()

    lane = lax.broadcasted_iota(jnp.int32, (channels, LANES), 1)

    def branches(b):
        here = slice(b * LANES, (b + 1) * LANES)
        now = nrm[:, here].astype(F32)
        before = halo[:, LANES:] if b == 0 else nrm[:, (b - 1) * LANES : b * LANES]
        before = before.astype(F32)
        shifted = [now]
        for t in (1, 2):
            shifted.append(
                jnp.where(lane < t, pltpu.roll(before, t, 1), pltpu.roll(now, t, 1))
            )
        total = []
        for n in range(3):
            total.append(sum(cols_ref[3 * n + t] * shifted[t] for t in range(3)))
        qbr[:, here] = total[0]
        pext[:, (b + 1) * LANES : (b + 2) * LANES] = (total[1] * total[2]).astype(BF16)

    halo_src = pext.at[:, pl.ds(blocks * LANES, 2 * LANES)]
    cp_halo = copy(halo_src, halo, R_HALO, R_HALO, c + 1)
    for n, q0 in enumerate(starts):
        cols = slice(q0, q0 + QB)
        total = ssq[0:1, cols]
        for d in range(1, n_f):
            ssq_copy(n, d).wait_recv()
            total = total + rssq[d - 1, 0:1, cols]
        scale = lax.rsqrt(total / (channels * n_f) + EPS)
        for b in range(q0 // LANES, (q0 + QB) // LANES):
            here = slice(b * LANES, (b + 1) * LANES)
            part = scale[:, b * LANES - q0 : (b + 1) * LANES - q0]
            nrm[:, here] = (att[:, here].astype(F32) * part * cols_ref[9]).astype(BF16)
        ready = range((q0 + QB) // LANES, q0 // LANES, -1)
        for b in ready:
            if b < blocks:
                branches(b)
            if b == blocks - 1:
                pext[:, (blocks + 1) * LANES :] = nrm[:, (blocks - 1) * LANES :]

                @pl.when(c + 1 < n_c)
                def _():
                    cp_halo.start()

    @pl.when(c >= 1)
    def _():
        copy(halo_src, halo, R_HALO, R_HALO, c - 1).wait_recv()

    @pl.when(c == 0)
    def _():
        halo[...] = jnp.zeros_like(halo)

    pext[:, :LANES] = halo[:, :LANES]
    branches(0)
    for pair in range(groups // 2):
        left = [
            pext[g * size : (g + 1) * size, b * LANES : (b + 2) * LANES]
            for g in (2 * pair, 2 * pair + 1)
            for b in range(blocks)
        ]
        long = jnp.dot(
            jnp.concatenate(left, axis=0), toep[pair], preferred_element_type=F32
        )
        for at in range(2 * blocks):
            g, b = 2 * pair + at // blocks, at % blocks
            ch = slice(g * size, (g + 1) * size)
            here = slice(b * LANES, (b + 1) * LANES)
            side = slice(at // blocks * LANES, (at // blocks + 1) * LANES)
            acc[ch, here] = (
                att[ch, here].astype(F32)
                + qbr[ch, here] * long[at * size : (at + 1) * size, side]
            )
        if (2 * pair + 2) * size % LANES == 0:
            j = (2 * pair + 2) * size // LANES - 1
            for b in range(blocks):
                piece = acc[j * LANES : (j + 1) * LANES, b * LANES : (b + 1) * LANES]
                out[b * LANES : (b + 1) * LANES, j * LANES : (j + 1) * LANES] = piece.T.astype(BF16)

    @pl.when(core0 & has_prev)
    def _():
        cp_q.wait_send()
        each_x((0, 1), low, lambda h, kind: x_copy(h, kind, c + 1, True).wait_send())

    @pl.when(core1 & has_prev)
    def _():
        each_x((0, 1), high, lambda h, kind: x_copy(h, kind, c - 1, True).wait_send())

    @pl.when(core0)
    def _():
        cp_yk.wait_send()
        cp_yv.wait_send()

    @pl.when(has_next0)
    def _():
        for n in range(n_q):
            for cp in o_copies(n, c + 2):
                cp.wait_send()

    @pl.when(has_next1)
    def _():
        each_x((0, 1), low, lambda h, kind: x_copy(h, kind, c + 1, False).wait_send())
        each_x((0, 1), high, lambda h, kind: x_copy(h, kind, c + 2, False).wait_send())

    for n in range(n_q):
        for d in range(1, n_f):
            ssq_copy(n, d).wait_send()

    @pl.when(c + 1 < n_c)
    def _():
        cp_halo.wait_send()


def per_device(n_c, n_f, queries, keys, values, norm_gain, short_filters, medium_filters):
    rows, channels = queries.shape
    heads = channels // HEAD
    groups = medium_filters.shape[1]
    sems = R_X + 2 * heads + (rows // QB) * (n_f + 1)
    hbm = pl.BlockSpec(memory_space=pltpu.HBM)
    vmem = pl.BlockSpec(memory_space=pltpu.VMEM)
    long = pltpu.VMEM((rows, channels), BF16)
    turned = pltpu.VMEM((channels, rows), BF16)
    stat = pltpu.VMEM((8, rows), F32)
    return pl.pallas_call(
        functools.partial(kernel, n_c, n_f),
        out_shape=jax.ShapeDtypeStruct((rows, channels), BF16),
        in_specs=[hbm] * 3 + [vmem] * 3,
        out_specs=vmem,
        scratch_shapes=[
            long, long, long,
            turned, long, turned, long, turned,
            long, turned, stat, turned, stat,
            pltpu.VMEM((channels, rows), F32), stat, stat,
            turned, stat, pltpu.VMEM((n_f - 1, 8, rows), F32),
            pltpu.VMEM((LANES, channels), F32),
            pltpu.VMEM((10, channels, LANES), F32),
            pltpu.VMEM((groups // 2, 2 * LANES, 2 * LANES), BF16),
            turned,
            pltpu.VMEM((channels, rows + 2 * LANES), BF16),
            pltpu.VMEM((channels, 2 * LANES), BF16),
            pltpu.VMEM((channels, rows), F32),
            pltpu.SemaphoreType.DMA((sems,)),
            pltpu.SemaphoreType.DMA((sems,)),
            pltpu.SemaphoreType.DMA((3 * rows // LANES,)),
        ],
        compiler_params=pltpu.CompilerParams(
            collective_id=0, has_side_effects=True, vmem_limit_bytes=55600 * 1024
        ),
    )(queries, keys, values, norm_gain.reshape(1, channels), short_filters, medium_filters.T)


def solution(mesh):
    placed = (
        P("ctx", "fsdp"),
        P("ctx", "fsdp"),
        P("ctx", "fsdp"),
        P("fsdp"),
        P(None, None, "fsdp"),
        P(None, "fsdp"),
    )
    return jax.shard_map(
        functools.partial(per_device, mesh.shape["ctx"], mesh.shape["fsdp"]),
        mesh=mesh, in_specs=placed, out_specs=P("ctx", "fsdp"), check_vma=False,
    )
```

```python
import functools
import math

import jax
import jax.numpy as jnp
from jax import lax
from jax.experimental import pallas as pl
from jax.experimental.pallas import tpu as pltpu
from jax.sharding import PartitionSpec as P

HEAD = 128
LANES = 128
QB = 256
EPS = 1e-06
BIG = -1e30
F32 = jnp.float32
BF16 = jnp.bfloat16
MESH = pl.DeviceIdType.MESH
NT = (((1,), (1,)), ((), ()))

R_Q, R_YK, R_YV, R_HALO, R_X = 0, 1, 2, 3, 4


def scores_of(q_ref, k_ref, h, q0, lo, hi, mode):
    lanes = slice(h * HEAD, (h + 1) * HEAD)
    s = lax.dot_general(
        k_ref[lo:hi, lanes], q_ref[q0 : q0 + QB, lanes], NT, preferred_element_type=F32
    ) * (math.log2(math.e) / math.sqrt(HEAD))
    if mode == "full":
        return s
    key = lax.broadcasted_iota(jnp.int32, (QB, QB), 0)
    query = lax.broadcasted_iota(jnp.int32, (QB, QB), 1)
    at = q0 - lo
    allowed = key <= query if mode == "causal" else key > query
    diag = jnp.where(allowed, s[at : at + QB], BIG)
    parts = ([s[:at]] if at else []) + [diag] + ([s[at + QB :]] if at + QB < hi - lo else [])
    return jnp.concatenate(parts, axis=0) if len(parts) > 1 else diag


def span(k_ref, q0, mode):
    rows = k_ref.shape[0]
    return {"full": (0, rows), "causal": (0, q0 + QB), "anti": (q0, rows)}[mode]


def pipelined(tasks):
    s = tasks[0][0]()
    for n, (_, finish) in enumerate(tasks):
        later = tasks[n + 1][0]() if n + 1 < len(tasks) else None
        finish(s)
        s = later


def softmax_task(q_ref, k_ref, vt_ref, h, q0, mode, old, write):
    lo, hi = span(k_ref, q0, mode)

    def finish(s):
        m = jnp.max(s, axis=0, keepdims=True)
        m_old = old()
        if m_old is not None:
            m = jnp.maximum(m, m_old)
        p = jnp.exp2(s - m)
        l = jnp.sum(p, axis=0, keepdims=True)
        o = jnp.dot(
            vt_ref[h * HEAD : (h + 1) * HEAD, lo:hi], p.astype(BF16), preferred_element_type=F32
        )
        write(m_old, m, l, o)

    return (lambda: scores_of(q_ref, k_ref, h, q0, lo, hi, mode)), finish


def attend(q_ref, k_ref, vt_ref, h, q0, mode, acc, m_ref, l_ref, first=False):
    cols = slice(q0, q0 + QB)
    ch = slice(h * HEAD, (h + 1) * HEAD)
    row = slice(h, h + 1)

    def write(m_old, m, l, o):
        if first:
            acc[ch, cols] = o
            l_ref[row, cols] = l
        else:
            a = jnp.exp2(m_old - m)
            acc[ch, cols] = acc[ch, cols] * a + o
            l_ref[row, cols] = l_ref[row, cols] * a + l
        m_ref[row, cols] = m

    old = (lambda: None) if first else (lambda: m_ref[row, cols])
    return softmax_task(q_ref, k_ref, vt_ref, h, q0, mode, old, write)


def kernel(
    n_c, n_f, q, k, v, gain, sf, mf, out,
    vt, xk, xvt, yk, yvt, rq, ot, ost, rot, rost, acc, m_ref, l_ref, att, ssq, rssq,
    wide, cols_ref, toep, nrm, pext, halo, qbr, send, recv,
):
    rows, channels = q.shape
    heads = channels // HEAD
    half = heads // 2
    groups = mf.shape[0]
    size = channels // groups
    blocks = rows // LANES
    n_q = rows // QB
    o_sem = R_X + 2 * heads + n_q * (n_f - 1)
    c = lax.axis_index("ctx")
    f = lax.axis_index("fsdp")
    core0 = lax.rem(c, 2) == 0
    core1 = lax.rem(c, 2) == 1
    has_prev = c >= 2
    has_next0 = core0 & (c + 2 < n_c)
    has_next1 = core1 & (c + 1 < n_c)

    def copy(src, dst, s, r, dc):
        return pltpu.make_async_remote_copy(
            src_ref=src, dst_ref=dst, send_sem=send.at[s], recv_sem=recv.at[r],
            device_id=(dc, f), device_id_type=MESH,
        )

    def x_parts(h):
        return (
            (xk.at[:, pl.ds(h * HEAD, HEAD)], k.at[:, pl.ds(h * HEAD, HEAD)]),
            (xvt.at[pl.ds(h * HEAD, HEAD)], vt.at[pl.ds(h * HEAD, HEAD)]),
        )

    def x_copy(h, kind, dc, forward):
        dst, own = x_parts(h)[kind]
        s = R_X + 2 * h + kind
        return copy(dst if forward else own, dst, s, s, dc)

    barrier = pltpu.get_barrier_semaphore()
    count = n_f - 1
    for d in range(1, n_f):
        pl.semaphore_signal(
            barrier, inc=1, device_id=(c, lax.rem(f + d, n_f)), device_id_type=MESH
        )
    for d in (1, 2):
        @pl.when(c >= d)
        def _():
            pl.semaphore_signal(barrier, inc=1, device_id=(c - d, f), device_id_type=MESH)

        @pl.when(c + d < n_c)
        def _():
            pl.semaphore_signal(barrier, inc=1, device_id=(c + d, f), device_id_type=MESH)

        count = count + jnp.where(c >= d, 1, 0) + jnp.where(c + d < n_c, 1, 0)
    pl.semaphore_wait(barrier, count)

    cp_q = copy(q, rq, R_Q, R_Q, c - 2)
    cp_yk = copy(k, yk, R_YK, R_YK, c + 1)
    cp_yv = copy(vt, yvt, R_YV, R_YV, c + 1)

    def o_copies(n, dc):
        piece = pl.ds(n_q * QB - (n + 1) * QB, QB)
        return (
            copy(ot.at[:, piece], rot.at[:, piece], o_sem + 2 * n, o_sem + 2 * n, dc),
            copy(ost.at[:, piece], rost.at[:, piece], o_sem + 2 * n + 1, o_sem + 2 * n + 1, dc),
        )

    @pl.when(core0 & has_prev)
    def _():
        cp_q.start()

    def each_x(kinds, which, act):
        for h in which:
            for kind in kinds:
                act(h, kind)

    low, high = range(half), range(half, heads)

    @pl.when(has_next1)
    def _():
        each_x((0,), low, lambda h, kind: x_copy(h, kind, c + 1, False).start())
        each_x((0,), high, lambda h, kind: x_copy(h, kind, c + 2, False).start())

    @pl.when(core0)
    def _():
        cp_yk.start()

    for b in range(blocks):
        for h in range(heads):
            piece = v[b * LANES : (b + 1) * LANES, h * HEAD : (h + 1) * HEAD].astype(F32)
            vt[h * HEAD : (h + 1) * HEAD, b * LANES : (b + 1) * LANES] = piece.T.astype(BF16)

    @pl.when(has_next1)
    def _():
        each_x((1,), low, lambda h, kind: x_copy(h, kind, c + 1, False).start())
        each_x((1,), high, lambda h, kind: x_copy(h, kind, c + 2, False).start())

    @pl.when(core0)
    def _():
        cp_yv.start()

    starts = list(range(0, rows, QB))[::-1]
    pipelined([
        attend(q, k, vt, h, q0, "causal", acc, m_ref, l_ref, first=True)
        for q0 in starts for h in range(heads)
    ])

    wide[...] = jnp.zeros_like(wide)
    for b in range(3):
        wide[3 * b : 3 * b + 3, :] = sf[b]
    wide[9:10, :] = gain[...]
    for j in range(channels // LANES):
        turned = wide[:, j * LANES : (j + 1) * LANES].T
        for n in range(10):
            cols_ref[n, j * LANES : (j + 1) * LANES, :] = jnp.broadcast_to(
                turned[:, n : n + 1], (LANES, LANES)
            )
    wide[:groups, :LANES] = mf[...].astype(F32)
    e = lax.broadcasted_iota(jnp.int32, (LANES, LANES), 0)
    i = lax.broadcasted_iota(jnp.int32, (LANES, LANES), 1)
    for g in range(groups):
        taps = jnp.broadcast_to(wide[g : g + 1, :LANES], (LANES, LANES))
        ring = pltpu.roll(taps, 0, 1, stride=1, stride_axis=0)
        side = slice(g % 2 * LANES, (g % 2 + 1) * LANES)
        toep[g // 2, :LANES, side] = jnp.where(i < e, ring, 0.0).astype(BF16)
        toep[g // 2, LANES:, side] = jnp.where(i >= e, ring, 0.0).astype(BF16)

    @pl.when(core1)
    def _():
        copy(k, yk, R_YK, R_YK, c - 1).wait_recv()
        copy(vt, yvt, R_YV, R_YV, c - 1).wait_recv()
        pipelined([
            attend(q, yk, yvt, h, q0, "full", acc, m_ref, l_ref)
            for q0 in starts for h in range(heads)
        ])

    @pl.when(has_next0)
    def _():
        copy(q, rq, R_Q, R_Q, c + 2).wait_recv()
        ost[...] = jnp.zeros_like(ost)

        def partial(n, h):
            cols = slice(starts[n], starts[n] + QB)

            def write(_, m, l, o):
                ot[h * HEAD : (h + 1) * HEAD, cols] = (o * (1.0 / l)).astype(BF16)
                ost[h : h + 1, cols] = m
                ost[heads + h : heads + h + 1, cols] = l
                if h == heads - 1:
                    for cp in o_copies(n, c + 2):
                        cp.start()

            return softmax_task(rq, k, vt, h, starts[n], "anti", lambda: None, write)

        pipelined([partial(n, h) for n in range(n_q) for h in range(heads)])

    def far_first(first_heads, other, mode):
        for h in first_heads:
            for kind in (0, 1):
                x_copy(h, kind, other, True).wait_recv()
                x_copy(h, kind, other, True).start()
        pipelined([
            attend(q, xk, xvt, h, q0, mode, acc, m_ref, l_ref)
            for q0 in starts for h in first_heads
        ])

    def far_later(later_heads, other, mode, n):
        for h in later_heads:
            if n == 0:
                for kind in (0, 1):
                    x_copy(h, kind, other, True).wait_recv()
        pipelined([
            attend(q, xk, xvt, h, starts[n], mode, acc, m_ref, l_ref) for h in later_heads
        ])

    @pl.when(core1 & has_prev)
    def _():
        far_first(high, c - 1, "anti")

    @pl.when(core0 & has_prev)
    def _():
        far_first(low, c + 1, "full")

    base = R_X + 2 * heads

    def ssq_copy(n, d):
        piece = pl.ds(starts[n], QB)
        s = base + n * (n_f - 1) + d - 1
        return pltpu.make_async_remote_copy(
            src_ref=ssq.at[:, piece], dst_ref=rssq.at[d - 1, :, piece], send_sem=send.at[s],
            recv_sem=recv.at[s], device_id=(c, lax.rem(f + d, n_f)), device_id_type=MESH,
        )

    for n, q0 in enumerate(starts):
        cols = slice(q0, q0 + QB)

        @pl.when(core1 & has_prev)
        def _():
            far_later(low, c - 1, "anti", n)

        @pl.when(core0 & has_prev)
        def _():
            far_later(high, c + 1, "full", n)
            for cp in o_copies(n, c - 2):
                cp.wait_recv()
            for h in range(heads):
                ch = slice(h * HEAD, (h + 1) * HEAD)
                m_old = m_ref[h : h + 1, cols]
                m_far = rost[h : h + 1, cols]
                m = jnp.maximum(m_old, m_far)
                a = jnp.exp2(m_old - m)
                b = jnp.exp2(m_far - m) * rost[heads + h : heads + h + 1, cols]
                acc[ch, cols] = acc[ch, cols] * a + rot[ch, cols].astype(F32) * b
                l_ref[h : h + 1, cols] = l_ref[h : h + 1, cols] * a + b

        squares = jnp.zeros((1, QB), F32)
        for h in range(heads):
            ch = slice(h * HEAD, (h + 1) * HEAD)
            done = (acc[ch, cols] * (1.0 / l_ref[h : h + 1, cols])).astype(BF16)
            att[ch, cols] = done
            done = done.astype(F32)
            squares = squares + jnp.sum(done * done, axis=0, keepdims=True)
        ssq[:, cols] = jnp.broadcast_to(squares, (8, QB))
        for d in range(1, n_f):
            ssq_copy(n, d).start()

    lane = lax.broadcasted_iota(jnp.int32, (channels, LANES), 1)

    def branches(b):
        here = slice(b * LANES, (b + 1) * LANES)
        now = nrm[:, here].astype(F32)
        before = halo[:, LANES:] if b == 0 else nrm[:, (b - 1) * LANES : b * LANES]
        before = before.astype(F32)
        shifted = [now]
        for t in (1, 2):
            shifted.append(
                jnp.where(lane < t, pltpu.roll(before, t, 1), pltpu.roll(now, t, 1))
            )
        total = []
        for n in range(3):
            total.append(sum(cols_ref[3 * n + t] * shifted[t] for t in range(3)))
        qbr[:, here] = total[0]
        pext[:, (b + 1) * LANES : (b + 2) * LANES] = (total[1] * total[2]).astype(BF16)

    halo_src = pext.at[:, pl.ds(blocks * LANES, 2 * LANES)]
    cp_halo = copy(halo_src, halo, R_HALO, R_HALO, c + 1)
    for n, q0 in enumerate(starts):
        cols = slice(q0, q0 + QB)
        total = ssq[0:1, cols]
        for d in range(1, n_f):
            ssq_copy(n, d).wait_recv()
            total = total + rssq[d - 1, 0:1, cols]
        scale = lax.rsqrt(total / (channels * n_f) + EPS)
        for b in range(q0 // LANES, (q0 + QB) // LANES):
            here = slice(b * LANES, (b + 1) * LANES)
            part = scale[:, b * LANES - q0 : (b + 1) * LANES - q0]
            nrm[:, here] = (att[:, here].astype(F32) * part * cols_ref[9]).astype(BF16)
        ready = range((q0 + QB) // LANES, q0 // LANES, -1)
        for b in ready:
            if b < blocks:
                branches(b)
            if b == blocks - 1:
                pext[:, (blocks + 1) * LANES :] = nrm[:, (blocks - 1) * LANES :]

                @pl.when(c + 1 < n_c)
                def _():
                    cp_halo.start()

    @pl.when(c >= 1)
    def _():
        copy(halo_src, halo, R_HALO, R_HALO, c - 1).wait_recv()

    @pl.when(c == 0)
    def _():
        halo[...] = jnp.zeros_like(halo)

    pext[:, :LANES] = halo[:, :LANES]
    branches(0)
    for pair in range(groups // 2):
        left = [
            pext[g * size : (g + 1) * size, b * LANES : (b + 2) * LANES]
            for g in (2 * pair, 2 * pair + 1)
            for b in range(blocks)
        ]
        long = jnp.dot(
            jnp.concatenate(left, axis=0), toep[pair], preferred_element_type=F32
        )
        for at in range(2 * blocks):
            g, b = 2 * pair + at // blocks, at % blocks
            ch = slice(g * size, (g + 1) * size)
            here = slice(b * LANES, (b + 1) * LANES)
            side = slice(at // blocks * LANES, (at // blocks + 1) * LANES)
            acc[ch, here] = (
                att[ch, here].astype(F32)
                + qbr[ch, here] * long[at * size : (at + 1) * size, side]
            )
        if (2 * pair + 2) * size % LANES == 0:
            j = (2 * pair + 2) * size // LANES - 1
            for b in range(blocks):
                piece = acc[j * LANES : (j + 1) * LANES, b * LANES : (b + 1) * LANES]
                out[b * LANES : (b + 1) * LANES, j * LANES : (j + 1) * LANES] = piece.T.astype(BF16)

    @pl.when(core0 & has_prev)
    def _():
        cp_q.wait_send()
        each_x((0, 1), low, lambda h, kind: x_copy(h, kind, c + 1, True).wait_send())

    @pl.when(core1 & has_prev)
    def _():
        each_x((0, 1), high, lambda h, kind: x_copy(h, kind, c - 1, True).wait_send())

    @pl.when(core0)
    def _():
        cp_yk.wait_send()
        cp_yv.wait_send()

    @pl.when(has_next0)
    def _():
        for n in range(n_q):
            for cp in o_copies(n, c + 2):
                cp.wait_send()

    @pl.when(has_next1)
    def _():
        each_x((0, 1), low, lambda h, kind: x_copy(h, kind, c + 1, False).wait_send())
        each_x((0, 1), high, lambda h, kind: x_copy(h, kind, c + 2, False).wait_send())

    for n in range(n_q):
        for d in range(1, n_f):
            ssq_copy(n, d).wait_send()

    @pl.when(c + 1 < n_c)
    def _():
        cp_halo.wait_send()


def per_device(n_c, n_f, queries, keys, values, norm_gain, short_filters, medium_filters):
    rows, channels = queries.shape
    heads = channels // HEAD
    groups = medium_filters.shape[1]
    sems = R_X + 2 * heads + (rows // QB) * (n_f + 1)
    vmem = pl.BlockSpec(memory_space=pltpu.VMEM)
    long = pltpu.VMEM((rows, channels), BF16)
    turned = pltpu.VMEM((channels, rows), BF16)
    stat = pltpu.VMEM((8, rows), F32)
    return pl.pallas_call(
        functools.partial(kernel, n_c, n_f),
        out_shape=jax.ShapeDtypeStruct((rows, channels), BF16),
        in_specs=[vmem] * 6,
        out_specs=vmem,
        scratch_shapes=[
            turned, long, turned, long, turned,
            long, turned, stat, turned, stat,
            pltpu.VMEM((channels, rows), F32), stat, stat,
            turned, stat, pltpu.VMEM((n_f - 1, 8, rows), F32),
            pltpu.VMEM((LANES, channels), F32),
            pltpu.VMEM((10, channels, LANES), F32),
            pltpu.VMEM((groups // 2, 2 * LANES, 2 * LANES), BF16),
            turned,
            pltpu.VMEM((channels, rows + 2 * LANES), BF16),
            pltpu.VMEM((channels, 2 * LANES), BF16),
            pltpu.VMEM((channels, rows), F32),
            pltpu.SemaphoreType.DMA((sems,)),
            pltpu.SemaphoreType.DMA((sems,)),
        ],
        compiler_params=pltpu.CompilerParams(
            collective_id=0, has_side_effects=True, vmem_limit_bytes=32 * 1024 * 1024
        ),
    )(queries, keys, values, norm_gain.reshape(1, channels), short_filters, medium_filters.T)


def solution(mesh):
    placed = (
        P("ctx", "fsdp"),
        P("ctx", "fsdp"),
        P("ctx", "fsdp"),
        P("fsdp"),
        P(None, None, "fsdp"),
        P(None, "fsdp"),
    )
    return jax.shard_map(
        functools.partial(per_device, mesh.shape["ctx"], mesh.shape["fsdp"]),
        mesh=mesh, in_specs=placed, out_specs=P("ctx", "fsdp"), check_vma=False,
    )
```
